32 devices in a mesh: blk: 8 (over z, y), rep: 4 (over x, core).
Axes of the slice: x: 2, y: 2, z: 4, core: 2. Of those that a mesh axis runs over, the one named last changes fastest.
Arguments:
- feats: bfloat16 [8192, 256], P(('blk', 'rep')), may hold values from -6 to 6
- weight: bfloat16 [256, 256], replicated, may hold values from -0.375 to 0.375
- bias: float32 [256], replicated, may hold values from -4 to 4
- grad_out: bfloat16 [8192, 256], P(('blk', 'rep')), may hold values from -6 to 6
- tile_values: bfloat16 [8, 4, 2, 64, 128, 128], P('blk', 'rep'), may hold values from -0.0625 to 0.0625
- tile_rows: int32 [8, 4, 2, 64], P('blk', 'rep'), may hold values from 0 to 7, as said below
- tile_cols: int32 [8, 4, 2, 64], P('blk', 'rep'), may hold values from 0 to 7, as said below
- tile_count: int32 [8, 4, 2], P('blk', 'rep'), may hold values from 32 to 64, as said below
Outputs:
- out: bfloat16 [8192, 256], P(('blk', 'rep'))
- grad_feats: bfloat16 [8192, 256], P(('blk', 'rep'))
- grad_weight: float32 [256, 256], P('rep')
- grad_bias: float32 [256], replicated
The draws below stay inside these ranges and needn't reach their ends.
Inputs may be any that keep to these rules, and one draw needn't show every extreme that they name: `tile_count`: some pair slot of some device holds exactly 64 live entries; slots past the count hold values that must be ignored. Within one pair slot the 64 entries name distinct (tile_rows, tile_cols) cells. `tile_cols`: see tile_rows: cells of one slot are distinct.
All inputs are finite; a program needn't handle non-finite values.
Results may differ from the reference program's by a relative error of at most 0.018.
Values may be sent and summed in bfloat16 or wider, within the bound.
A program may use at most 64 MiB of HBM per device.

```python
import jax
import jax.numpy as jnp
from jax import lax

F = 256
TILE = 128
MAXT = 64
TILES_P = 8
ROWS_DEV = 256
PAIRS_DEV = 2
NODES = 8192
N_BLK = 8
N_REP = 4


def draw_tile_count(key, part):
    first_key, second_key = jax.random.split(jax.random.fold_in(key, 17))
    entries = N_BLK * N_REP * PAIRS_DEV
    counts = jax.random.randint(first_key, (entries,), MAXT // 2, MAXT + 1, dtype=jnp.int32)
    chosen = jax.random.randint(second_key, (), 0, entries, dtype=jnp.int32)
    counts = counts.at[chosen].set(MAXT)
    return counts.reshape(N_BLK, N_REP, PAIRS_DEV)


def tile_cells(key):
    first_key, second_key = jax.random.split(jax.random.fold_in(key, 23))
    slot_total = N_BLK * N_REP * PAIRS_DEV
    cell_total = TILES_P * TILES_P
    cell_index = jnp.arange(cell_total, dtype=jnp.int32)
    scores = jax.random.randint(first_key, (slot_total, cell_total), 0, 2 ** 20, dtype=jnp.int32)
    scores = scores * cell_total + cell_index[None, :]
    chosen = jax.random.randint(second_key, (), 0, slot_total, dtype=jnp.int32)
    slot_index = jnp.arange(slot_total, dtype=jnp.int32)
    planted = (slot_index[:, None] == chosen) & ((cell_index == 0) | (cell_index == cell_total - 1))[None, :]
    scores = jnp.where(planted, (cell_index - cell_total)[None, :], scores)
    order = jnp.argsort(scores, axis=1)[:, :MAXT].astype(jnp.int32)
    return order.reshape(N_BLK, N_REP, PAIRS_DEV, MAXT)


def draw_tile_rows(key, part):
    return tile_cells(key) // TILES_P


def draw_tile_cols(key, part):
    return tile_cells(key) % TILES_P


def levels(stream_key, shape, cuts, low, high):
    loudness = 1.0
    for dim, blocks in cuts:
        draws = jax.random.uniform(jax.random.fold_in(jax.random.fold_in(stream_key, 6), dim), (blocks,), jnp.float32, low / len(cuts), high / len(cuts))
        loudness = loudness * jnp.repeat(jnp.exp(draws), shape[dim] // blocks).reshape((-1,) + (1,) * (len(shape) - 1 - dim))
    return loudness


def scatter_about(stream_key, extent, width, reach, pieces=(), held_as=jnp.bfloat16):
    values = jax.random.normal(stream_key, extent, jnp.float32) * width
    if len(pieces) > 0:
        values = levels(stream_key, extent, pieces, -0.22, 0.18) * values
    return jnp.clip(values, min=-reach, max=reach).astype(held_as)


def setup_inputs(seed: int = 0) -> dict:
    seeds = jax.random.split(jax.random.key(seed), 9)
    feats = scatter_about(seeds[0], (NODES, F), 1.0, 6.0, ((0, 32),))
    weight = scatter_about(seeds[1], (F, F), F ** -0.5, 0.375)
    bias = scatter_about(seeds[2], (F,), 1.0, 4.0, (), jnp.float32)
    grad_out = scatter_about(seeds[3], (NODES, F), 1.0, 6.0, ((0, 32),))
    tile_values = scatter_about(seeds[4], (N_BLK, N_REP, PAIRS_DEV, MAXT, TILE, TILE), (TILE * MAXT * N_BLK // TILES_P) ** -0.5, 0.0625, ((0, 8), (1, 4)))
    tile_rows = draw_tile_rows(jax.random.fold_in(seeds[8], 71), 0)
    tile_cols = draw_tile_cols(jax.random.fold_in(seeds[8], 71), 0)
    tile_count = draw_tile_count(jax.random.fold_in(seeds[8], 71), 0)
    return {"feats": feats, "weight": weight, "bias": bias, "grad_out": grad_out, "tile_values": tile_values, "tile_rows": tile_rows, "tile_cols": tile_cols, "tile_count": tile_count}


def forward_tiles(total, source, tile_vals, tile_row, tile_col, live, tile_size):
    def one_tile(position, total):
        row_start = tile_row[position] * tile_size
        col_start = tile_col[position] * tile_size
        source_rows = lax.dynamic_slice_in_dim(source, col_start, tile_size, 0)
        current = lax.dynamic_slice_in_dim(total, row_start, tile_size, 0)
        current = current + jnp.dot(tile_vals[position], source_rows, preferred_element_type=jnp.float32)
        return lax.dynamic_update_slice_in_dim(total, current, row_start, 0)
    return lax.fori_loop(0, live, one_tile, total)


def reference(feats, weight, bias, grad_out, tile_values, tile_rows, tile_cols, tile_count):
    part_rows = ROWS_DEV * N_REP
    pair_total = N_REP * PAIRS_DEV
    hw_full = jnp.dot(feats, weight, preferred_element_type=jnp.float32).astype(jnp.bfloat16)
    hw_blocks = hw_full.reshape(N_BLK, part_rows, F)

    def forward_part(part_index):
        def pair_step(total, flat):
            replica = flat // PAIRS_DEV
            slot = flat % PAIRS_DEV
            source_part = (part_index - replica - slot * N_REP) % N_BLK
            source = lax.dynamic_index_in_dim(hw_blocks, source_part, 0, keepdims=False)
            total = forward_tiles(total, source, tile_values[part_index, replica, slot],
                                  tile_rows[part_index, replica, slot], tile_cols[part_index, replica, slot],
                                  tile_count[part_index, replica, slot], TILE)
            return total, None
        total, _ = lax.scan(pair_step, jnp.zeros((part_rows, F), jnp.float32), jnp.arange(pair_total, dtype=jnp.int32))
        return total

    aggregate = lax.map(forward_part, jnp.arange(N_BLK, dtype=jnp.int32)).reshape(NODES, F)
    pre_act = aggregate + bias
    logistic = jax.nn.sigmoid(pre_act)
    out = (pre_act * logistic).astype(jnp.bfloat16)
    grad_pre = (grad_out.astype(jnp.float32) * logistic * (1.0 + pre_act * (1.0 - logistic))).astype(jnp.bfloat16)

    def backward_step(total, flat):
        part_index = flat // pair_total
        pair_flat = flat % pair_total
        replica = pair_flat // PAIRS_DEV
        slot = pair_flat % PAIRS_DEV
        source_part = (part_index - replica - slot * N_REP) % N_BLK
        tile_vals = tile_values[part_index, replica, slot]
        tile_row = tile_rows[part_index, replica, slot]
        tile_col = tile_cols[part_index, replica, slot]

        def one_tile(position, total):
            row_start = part_index * part_rows + tile_row[position] * TILE
            col_start = source_part * part_rows + tile_col[position] * TILE
            grad_rows = lax.dynamic_slice_in_dim(grad_pre, row_start, TILE, 0)
            term = lax.dot_general(tile_vals[position], grad_rows, (((0,), (0,)), ((), ())),
                                   preferred_element_type=jnp.float32)
            current = lax.dynamic_slice_in_dim(total, col_start, TILE, 0)
            return lax.dynamic_update_slice_in_dim(total, current + term, col_start, 0)
        total = lax.fori_loop(0, tile_count[part_index, replica, slot], one_tile, total)
        return total, None

    grad_total, _ = lax.scan(backward_step, jnp.zeros((NODES, F), jnp.float32),
                             jnp.arange(N_BLK * pair_total, dtype=jnp.int32))
    grad_hw = grad_total.astype(jnp.bfloat16)
    grad_feats = lax.dot_general(grad_hw, weight, (((1,), (1,)), ((), ())),
                                 preferred_element_type=jnp.float32).astype(jnp.bfloat16)
    grad_weight = lax.dot_general(feats, grad_hw, (((0,), (0,)), ((), ())), preferred_element_type=jnp.float32)
    grad_bias = jnp.sum(grad_pre.astype(jnp.float32), axis=0)
    return (out, grad_feats, grad_weight, grad_bias)
```

```python
import functools

import jax
import jax.numpy as jnp
from jax import lax
from jax.experimental import pallas as pl
from jax.experimental.pallas import tpu as pltpu
from jax.sharding import PartitionSpec as P

MESH = pl.DeviceIdType.MESH
UNIT = 256
CHUNK = 16
HALF = 128


def remote(src, dst, send, recv, blk, rep):
    return pltpu.make_async_remote_copy(
        src_ref=src, dst_ref=dst, send_sem=send, recv_sem=recv, device_id=(blk, rep), device_id_type=MESH
    )


def layer_kernel(
    n_blk, n_rep, n_slot, tile, cells, tiles_side,
    inv_ref, feats_ref, weight_ref, bias_ref, gout_ref, tiles_hbm,
    out_ref, gf_ref, gw_ref, gb_ref,
    tiles, dense, hw, hwbuf, acc, part, aggbuf, gbuf, g_t, pbuf, ghbuf, feats_t,
    bias_mine, bias_buf, terms, wbuf, wsum, fin,
    tile_sem, hw_send, hw_recv, rs_send, rs_recv, ag_send, ag_recv, bw_send, bw_recv,
    bias_send, bias_recv, w_send, w_recv, fin_send, fin_recv,
):
    n_dev = n_blk * n_rep
    rows = feats_ref.shape[0]
    units = rows * n_rep // UNIT
    per = UNIT // rows
    width = feats_ref.shape[1]
    w_rows = width // n_rep
    owners = (w_rows // CHUNK) * (width // HALF)
    halves = width // HALF
    me_b = lax.axis_index("blk")
    me_r = lax.axis_index("rep")
    me = me_b * n_rep + me_r

    barrier = pltpu.get_barrier_semaphore()

    def greet(d, carry):
        other = lax.rem(me + d, n_dev)
        pl.semaphore_signal(
            barrier, inc=1, device_id=(other // n_rep, lax.rem(other, n_rep)), device_id_type=MESH
        )
        return carry

    lax.fori_loop(1, n_dev, greet, 0)

    loads = []
    for k in range(n_slot):
        span = pl.ds(k * cells, cells)
        load = pltpu.make_async_copy(tiles_hbm.at[span], tiles.at[span], tile_sem.at[k])
        load.start()
        loads.append(load)
    hw[...] = jnp.dot(
        feats_ref[...], weight_ref[...], preferred_element_type=jnp.float32
    ).astype(jnp.bfloat16)
    pl.semaphore_wait(barrier, n_dev - 1)

    def hw_copy(k, r):
        to = lax.rem(me_b + r + n_rep * k, n_blk)
        return remote(hw, hwbuf.at[k, me_r], hw_send.at[k, r], hw_recv.at[k, me_r], to, r)

    for k in range(n_slot):
        for r in range(n_rep):
            if k == 0 and r == 0:
                @pl.when(me_r != 0)
                def _():
                    hw_copy(0, 0).start()

                @pl.when(me_r == 0)
                def _():
                    hwbuf[0, 0] = hw[...]
            else:
                hw_copy(k, r).start()

    tiles[n_slot * cells] = jnp.zeros((tile, tile), jnp.bfloat16)
    for load in loads:
        load.wait()
    for k in range(n_slot):
        def fill(r, carry, k=k):
            for c in range(tiles_side):
                entry = inv_ref[k * tiles_side * tiles_side + r * tiles_side + c]
                dense[k, pl.ds(pl.multiple_of(r * tile, tile), tile), c * tile:(c + 1) * tile] = tiles[entry]
            return carry

        lax.fori_loop(0, tiles_side, fill, 0)
    feats_t[...] = feats_ref[...].T

    def hw_wait(k, src):
        remote(hw, hwbuf.at[k, src], hw_send.at[k, src], hw_recv.at[k, src], me_b, me_r).wait_recv()

    def rs_copy(j):
        return remote(part.at[j], aggbuf.at[me_r], rs_send.at[j], rs_recv.at[me_r], me_b, j)

    for k in range(n_slot):
        for u in range(units):
            for i in range(per):
                src = u * per + i
                if k == 0 and src == 0:
                    @pl.when(me_r != 0)
                    def _():
                        hw_wait(0, 0)
                else:
                    hw_wait(k, src)
            rhs = hwbuf[k, u * per:(u + 1) * per].reshape(UNIT, width)
            last = k == n_slot - 1 and u == units - 1
            for j in range(units):
                at = slice(j * UNIT, (j + 1) * UNIT)
                got = jnp.dot(
                    dense[k, at, u * UNIT:(u + 1) * UNIT], rhs, preferred_element_type=jnp.float32
                )
                if k + u > 0:
                    got = got + acc[at]
                acc[at] = got
                if last:
                    part[j * per:(j + 1) * per] = got.astype(jnp.bfloat16).reshape(per, rows, width)
                    for i in range(per):
                        @pl.when(me_r != j * per + i)
                        def _():
                            rs_copy(j * per + i).start()

    total = acc[pl.ds(pl.multiple_of(me_r * rows, rows), rows)]
    for d in range(1, n_rep):
        src = lax.rem(me_r + d, n_rep)
        remote(
            part.at[0], aggbuf.at[src], rs_send.at[src], rs_recv.at[src], me_b, src
        ).wait_recv()
        total = total + aggbuf[src].astype(jnp.float32)

    pre = total + bias_ref[...]
    logistic = jax.nn.sigmoid(pre)
    grad = (gout_ref[...].astype(jnp.float32) * logistic * (1.0 + pre * (1.0 - logistic))).astype(jnp.bfloat16)
    gbuf[me_r] = grad

    def ag_copy(d):
        to = lax.rem(me_r + d, n_rep)
        return remote(gbuf.at[me_r], gbuf.at[me_r], ag_send.at[d], ag_recv.at[me_r], me_b, to)

    for d in range(1, n_rep):
        ag_copy(d).start()
    out_ref[...] = (pre * logistic).astype(jnp.bfloat16)
    for d in range(1, n_rep):
        src = lax.rem(me_r + d, n_rep)
        remote(gbuf.at[src], gbuf.at[src], ag_send.at[d], ag_recv.at[src], me_b, src).wait_recv()
    for u in range(units):
        g_t[:, u * UNIT:(u + 1) * UNIT] = gbuf[u * per:(u + 1) * per].reshape(UNIT, width).T

    def bw_copy(k, j):
        to = lax.rem(me_b - me_r - n_rep * k + 2 * n_blk, n_blk)
        slot = k * n_rep + me_r
        return remote(pbuf.at[k, j], ghbuf.at[slot], bw_send.at[k, j], bw_recv.at[slot], to, j)

    for k in reversed(range(n_slot)):
        for u in range(units):
            term = jnp.dot(
                g_t[...], dense[k, :, u * UNIT:(u + 1) * UNIT], preferred_element_type=jnp.float32
            )
            pbuf[k, u * per:(u + 1) * per] = term.T.astype(jnp.bfloat16).reshape(per, rows, width)
            for i in range(per):
                j = u * per + i
                if k == 0 and j == 0:
                    @pl.when(me_r != 0)
                    def _():
                        bw_copy(0, 0).start()

                    @pl.when(me_r == 0)
                    def _():
                        ghbuf[0] = pbuf[0, 0]
                else:
                    bw_copy(k, j).start()

    bias_mine[...] = jnp.dot(
        jnp.ones((8, rows * n_rep), jnp.bfloat16),
        gbuf[...].reshape(rows * n_rep, width),
        preferred_element_type=jnp.float32,
    )

    def bias_send_one(d, carry):
        to = lax.rem(me_b + d, n_blk)
        remote(bias_mine, bias_buf.at[n_blk - 1 - d], bias_send, bias_recv, to, me_r).start()
        return carry

    lax.fori_loop(1, n_blk, bias_send_one, 0)

    total = jnp.zeros((rows, width), jnp.float32)
    for k in reversed(range(n_slot)):
        for r in range(n_rep):
            slot = k * n_rep + r

            def arrived():
                remote(
                    pbuf.at[0, 0], ghbuf.at[slot], bw_send.at[k, r], bw_recv.at[slot], me_b, me_r
                ).wait_recv()

            if slot == 0:
                pl.when(me_r != 0)(arrived)
            else:
                arrived()
            total = total + ghbuf[slot].astype(jnp.float32)
    gh = total.astype(jnp.bfloat16)
    w_terms = jnp.dot(feats_t[...], gh, preferred_element_type=jnp.float32).astype(jnp.bfloat16)
    for h in range(halves):
        terms[h] = w_terms[:, h * HALF:(h + 1) * HALF]

    def chunk_of(b, r):
        return terms.at[lax.rem(b, halves), pl.ds(pl.multiple_of(r * w_rows + b // halves * CHUNK, CHUNK), CHUNK)]

    def w_send_one(d, carry):
        other = lax.rem(me + d, n_dev)
        b, r = other // n_rep, lax.rem(other, n_rep)

        def go():
            remote(chunk_of(b, r), wbuf.at[n_dev - 1 - d], w_send, w_recv, b, r).start()

        if owners == n_blk:
            go()
        else:
            pl.when(b < owners)(go)
        return carry

    lax.fori_loop(1, n_dev, w_send_one, 0)
    gf_ref[...] = lax.dot_general(
        gh, weight_ref[...], (((1,), (1,)), ((), ())), preferred_element_type=jnp.float32
    ).astype(jnp.bfloat16)
    all_bias = bias_buf
    remote(all_bias, all_bias, bias_send, bias_recv, me_b, me_r).wait_recv()
    gb_ref[...] = (bias_mine[...] + jnp.sum(bias_buf[...], axis=0))[0:1]

    def fin_copy(d):
        to = lax.rem(me_b + d, n_blk)
        return remote(wsum, fin.at[me_b], fin_send.at[d], fin_recv.at[me_b], to, me_r)

    def own_chunk():
        remote(wbuf, wbuf, w_send, w_recv, me_b, me_r).wait_recv()
        mine = terms[
            lax.rem(me_b, halves), pl.ds(pl.multiple_of(me_r * w_rows + me_b // halves * CHUNK, CHUNK), CHUNK)
        ]
        wsum[...] = mine.astype(jnp.float32) + jnp.sum(wbuf[...].astype(jnp.float32), axis=0)
        for d in range(1, n_blk):
            fin_copy(d).start()
        fin[me_b] = wsum[...]

    if owners == n_blk:
        own_chunk()
    else:
        pl.when(me_b < owners)(own_chunk)
    for o in range(owners):
        @pl.when(me_b != o)
        def _():
            remote(wsum, fin.at[o], fin_send.at[0], fin_recv.at[o], me_b, me_r).wait_recv()

        at = o // halves * CHUNK
        gw_ref[at:at + CHUNK, (o % halves) * HALF:(o % halves + 1) * HALF] = fin[o]

    for k in range(n_slot):
        for r in range(n_rep):
            if k == 0 and r == 0:
                @pl.when(me_r != 0)
                def _():
                    hw_copy(0, 0).wait_send()
                    bw_copy(0, 0).wait_send()
            else:
                hw_copy(k, r).wait_send()
                bw_copy(k, r).wait_send()
    for j in range(n_rep):
        @pl.when(me_r != j)
        def _():
            rs_copy(j).wait_send()
    for d in range(1, n_rep):
        ag_copy(d).wait_send()
    remote(all_bias, all_bias, bias_send, bias_recv, me_b, me_r).wait_send()
    if owners == n_blk:
        remote(wbuf, wbuf, w_send, w_recv, me_b, me_r).wait_send()
    else:
        def w_left(d, carry):
            other = lax.rem(me + d, n_dev)

            @pl.when(other // n_rep < owners)
            def _():
                remote(wbuf.at[0], wbuf.at[0], w_send, w_recv, me_b, me_r).wait_send()
            return carry

        lax.fori_loop(1, n_dev, w_left, 0)

    def fin_left():
        for d in range(1, n_blk):
            fin_copy(d).wait_send()

    if owners == n_blk:
        fin_left()
    else:
        pl.when(me_b < owners)(fin_left)


def body(feats, weight, bias, grad_out, tile_values, tile_rows, tile_cols, tile_count):
    n_blk = lax.axis_size("blk")
    n_rep = lax.axis_size("rep")
    n_slot, cells, tile = tile_values.shape[2:5]
    rows, width = feats.shape
    n_dev = n_blk * n_rep
    part_rows = rows * n_rep
    side = part_rows // tile
    w_rows = width // n_rep
    owners = (w_rows // CHUNK) * (width // HALF)

    named = tile_rows[0, 0] * side + tile_cols[0, 0]
    live = jnp.arange(cells, dtype=jnp.int32)[None] < tile_count[0, 0][:, None]
    entry = jnp.arange(n_slot * cells, dtype=jnp.int32).reshape(n_slot, cells)
    hit = (named[:, None, :] == jnp.arange(side * side, dtype=jnp.int32)[None, :, None]) & live[:, None, :]
    inv = jnp.min(jnp.where(hit, entry[:, None, :], n_slot * cells), axis=2).reshape(-1)

    bf16, f32 = jnp.bfloat16, jnp.float32
    vmem = pl.BlockSpec(memory_space=pltpu.VMEM)
    dma = pltpu.SemaphoreType.DMA
    out, gf, gw, gb = pl.pallas_call(
        functools.partial(layer_kernel, n_blk, n_rep, n_slot, tile, cells, side),
        out_shape=(
            jax.ShapeDtypeStruct((rows, width), bf16),
            jax.ShapeDtypeStruct((rows, width), bf16),
            jax.ShapeDtypeStruct((w_rows, width), f32),
            jax.ShapeDtypeStruct((1, width), f32),
        ),
        in_specs=[pl.BlockSpec(memory_space=pltpu.SMEM), vmem, vmem, vmem, vmem, pl.BlockSpec(memory_space=pl.ANY)],
        out_specs=(vmem, vmem, vmem, vmem),
        scratch_shapes=[
            pltpu.VMEM((n_slot * cells + 1, tile, tile), bf16),
            pltpu.VMEM((n_slot, part_rows, part_rows), bf16),
            pltpu.VMEM((rows, width), bf16),
            pltpu.VMEM((n_slot, n_rep, rows, width), bf16),
            pltpu.VMEM((part_rows, width), f32),
            pltpu.VMEM((n_rep, rows, width), bf16),
            pltpu.VMEM((n_rep, rows, width), bf16),
            pltpu.VMEM((n_rep, rows, width), bf16),
            pltpu.VMEM((width, part_rows), bf16),
            pltpu.VMEM((n_slot, n_rep, rows, width), bf16),
            pltpu.VMEM((n_slot * n_rep, rows, width), bf16),
            pltpu.VMEM((width, rows), bf16),
            pltpu.VMEM((8, width), f32),
            pltpu.VMEM((n_blk - 1, 8, width), f32),
            pltpu.VMEM((width // HALF, width, HALF), bf16),
            pltpu.VMEM((n_dev - 1, CHUNK, HALF), bf16),
            pltpu.VMEM((CHUNK, HALF), f32),
            pltpu.VMEM((owners, CHUNK, HALF), f32),
            dma((n_slot,)),
            dma((n_slot, n_rep)),
            dma((n_slot, n_rep)),
            dma((n_rep,)),
            dma((n_rep,)),
            dma((n_rep,)),
            dma((n_rep,)),
            dma((n_slot, n_rep)),
            dma((n_slot * n_rep,)),
            dma,
            dma,
            dma,
            dma,
            dma((n_blk,)),
            dma((owners,)),
        ],
        compiler_params=pltpu.CompilerParams(
            collective_id=0, has_side_effects=True, vmem_limit_bytes=40 * 2 ** 20
        ),
        name="graph_layer",
    )(inv, feats, weight, bias.reshape(1, width), grad_out, tile_values.reshape(n_slot * cells, tile, tile))
    return (out, gf, gw, gb.reshape(width))


def solution(mesh):
    in_specs = (
        P(("blk", "rep"), None),
        P(),
        P(),
        P(("blk", "rep"), None),
        P("blk", "rep", None, None, None, None),
        P("blk", "rep", None, None),
        P("blk", "rep", None, None),
        P("blk", "rep", None),
    )
    out_specs = (P(("blk", "rep"), None), P(("blk", "rep"), None), P("rep", None), P())
    return jax.shard_map(body, mesh=mesh, in_specs=in_specs, out_specs=out_specs, check_vma=False)
```

```python
import functools

import jax
import jax.numpy as jnp
from jax import lax
from jax.experimental import pallas as pl
from jax.experimental.pallas import tpu as pltpu
from jax.sharding import PartitionSpec as P

MESH = pl.DeviceIdType.MESH
UNIT = 256
CHUNK = 16
HALF = 128


def remote(src, dst, send, recv, blk, rep):
    return pltpu.make_async_remote_copy(
        src_ref=src, dst_ref=dst, send_sem=send, recv_sem=recv, device_id=(blk, rep), device_id_type=MESH
    )


def layer_kernel(
    n_blk, n_rep, n_slot, tile, cells, tiles_side,
    inv_ref, feats_hbm, weight_hbm, bias_hbm, gout_hbm, tiles_hbm,
    out_ref, gf_ref, gw_ref, gb_ref,
    feats_ref, weight_ref, bias_ref, gout_ref, tiles, dense, hw, hw_other, hwbuf, acc, part, aggbuf, gbuf, g_t, pbuf, ghbuf, feats_t,
    cross, bias_mine, bias_buf, terms, wbuf, wsum, fin,
    in_sem, tile_sem, swap_send, swap_recv, cross_send, cross_recv, hw_send, hw_recv, rs_send, rs_recv, ag_send, ag_recv, bw_send, bw_recv,
    bias_send, bias_recv, w_send, w_recv, fin_send, fin_recv,
):
    n_dev = n_blk * n_rep
    rows = feats_ref.shape[0]
    units = rows * n_rep // UNIT
    per = UNIT // rows
    width = feats_ref.shape[1]
    w_rows = width // n_rep
    owners = (w_rows // CHUNK) * (width // HALF)
    halves = width // HALF
    me_b = lax.axis_index("blk")
    me_r = lax.axis_index("rep")
    me = me_b * n_rep + me_r
    half = me_b // n_rep
    place = lax.rem(me_b, n_rep)
    partner = lax.rem(me_b + n_rep, n_blk)
    near_slot = jnp.where(place < me_r, 1, 0)

    small = []
    for i, (src, dst) in enumerate(
        ((feats_hbm, feats_ref), (weight_hbm, weight_ref), (bias_hbm, bias_ref), (gout_hbm, gout_ref))
    ):
        small.append(pltpu.make_async_copy(src, dst, in_sem.at[i]))
        small[-1].start()
    loads = []
    for k in range(n_slot):
        span = pl.ds(k * cells, cells)
        load = pltpu.make_async_copy(tiles_hbm.at[span], tiles.at[span], tile_sem.at[k])
        load.start()
        loads.append(load)
    barrier = pltpu.get_barrier_semaphore()

    def greet(d, carry):
        other = lax.rem(me + d, n_dev)
        pl.semaphore_signal(
            barrier, inc=1, device_id=(other // n_rep, lax.rem(other, n_rep)), device_id_type=MESH
        )
        return carry

    lax.fori_loop(1, n_dev, greet, 0)

    small[0].wait()
    small[1].wait()
    hw[...] = jnp.dot(
        feats_ref[...], weight_ref[...], preferred_element_type=jnp.float32
    ).astype(jnp.bfloat16)
    pl.semaphore_wait(barrier, n_dev - 1)

    swap = remote(hw, hw_other, swap_send, swap_recv, partner, me_r)
    swap.start()

    def hw_copy(h, r):
        to = half * n_rep + lax.rem(place + r, n_rep)
        src = hw if h == 0 else hw_other
        return remote(src, hwbuf.at[h, me_r], hw_send.at[h, r], hw_recv.at[h, me_r], to, r)

    def hw_share(h):
        for r in reversed(range(n_rep)):
            if r == 0:
                @pl.when(me_r != 0)
                def _():
                    hw_copy(h, 0).start()

                @pl.when(me_r == 0)
                def _():
                    hwbuf[h, 0] = hw[...] if h == 0 else hw_other[...]
            else:
                hw_copy(h, r).start()

    hw_share(0)

    tiles[n_slot * cells] = jnp.zeros((tile, tile), jnp.bfloat16)
    for load in loads:
        load.wait()
    for h in range(2):
        base = jnp.where(near_slot == 1, 1 - h, h) * tiles_side * tiles_side

        def fill(r, carry, h=h, base=base):
            for c in range(tiles_side):
                entry = inv_ref[base + r * tiles_side + c]
                dense[h, pl.ds(pl.multiple_of(r * tile, tile), tile), c * tile:(c + 1) * tile] = tiles[entry]
            return carry

        lax.fori_loop(0, tiles_side, fill, 0)
        if h == 0:
            swap.wait_recv()
            hw_share(1)
    feats_t[...] = feats_ref[...].T

    def hw_wait(k, src):
        remote(hw, hwbuf.at[k, src], hw_send.at[k, src], hw_recv.at[k, src], me_b, me_r).wait_recv()

    def rs_copy(j):
        return remote(part.at[j], aggbuf.at[me_r], rs_send.at[j], rs_recv.at[me_r], me_b, j)

    for k in range(n_slot):
        for u in range(units):
            for i in range(per):
                src = u * per + i
                if src == 0:
                    @pl.when(me_r != 0)
                    def _():
                        hw_wait(k, 0)
                else:
                    hw_wait(k, src)
            rhs = hwbuf[k, u * per:(u + 1) * per].reshape(UNIT, width)
            last = k == n_slot - 1 and u == units - 1
            for j in range(units):
                at = slice(j * UNIT, (j + 1) * UNIT)
                got = jnp.dot(
                    dense[k, at, u * UNIT:(u + 1) * UNIT], rhs, preferred_element_type=jnp.float32
                )
                if k + u > 0:
                    got = got + acc[at]
                acc[at] = got
                if last:
                    part[j * per:(j + 1) * per] = got.astype(jnp.bfloat16).reshape(per, rows, width)
                    for i in range(per):
                        @pl.when(me_r != j * per + i)
                        def _():
                            rs_copy(j * per + i).start()

    total = acc[pl.ds(pl.multiple_of(me_r * rows, rows), rows)]
    for d in range(1, n_rep):
        src = lax.rem(me_r + d, n_rep)
        remote(
            part.at[0], aggbuf.at[src], rs_send.at[src], rs_recv.at[src], me_b, src
        ).wait_recv()
        total = total + aggbuf[src].astype(jnp.float32)

    small[2].wait()
    small[3].wait()
    pre = total + bias_ref[...]
    logistic = jax.nn.sigmoid(pre)
    grad = (gout_ref[...].astype(jnp.float32) * logistic * (1.0 + pre * (1.0 - logistic))).astype(jnp.bfloat16)
    gbuf[me_r] = grad

    def ag_copy(d):
        to = lax.rem(me_r + d, n_rep)
        return remote(gbuf.at[me_r], gbuf.at[me_r], ag_send.at[d], ag_recv.at[me_r], me_b, to)

    for d in range(1, n_rep):
        ag_copy(d).start()
    out_ref[...] = (pre * logistic).astype(jnp.bfloat16)
    for d in range(1, n_rep):
        src = lax.rem(me_r + d, n_rep)
        remote(gbuf.at[src], gbuf.at[src], ag_send.at[d], ag_recv.at[src], me_b, src).wait_recv()
    for u in range(units):
        g_t[:, u * UNIT:(u + 1) * UNIT] = gbuf[u * per:(u + 1) * per].reshape(UNIT, width).T

    def bw_copy(k, j):
        to = half * n_rep + lax.rem(place - me_r + n_rep, n_rep)
        slot = k * n_rep + me_r
        return remote(pbuf.at[k, j], ghbuf.at[slot], bw_send.at[k, j], bw_recv.at[slot], to, j)

    for k in reversed(range(n_slot)):
        for u in range(units):
            term = jnp.dot(
                g_t[...], dense[k, :, u * UNIT:(u + 1) * UNIT], preferred_element_type=jnp.float32
            )
            pbuf[k, u * per:(u + 1) * per] = term.T.astype(jnp.bfloat16).reshape(per, rows, width)
            for i in range(per):
                j = u * per + i
                if j == 0:
                    @pl.when(me_r != 0)
                    def _():
                        bw_copy(k, 0).start()

                    @pl.when(me_r == 0)
                    def _():
                        ghbuf[k * n_rep] = pbuf[k, 0]
                else:
                    bw_copy(k, j).start()

    bias_mine[...] = jnp.dot(
        jnp.ones((8, rows * n_rep), jnp.bfloat16),
        gbuf[...].reshape(rows * n_rep, width),
        preferred_element_type=jnp.float32,
    )

    def bias_send_one(d, carry):
        to = lax.rem(me_b + d, n_blk)
        remote(bias_mine, bias_buf.at[n_blk - 1 - d], bias_send, bias_recv, to, me_r).start()
        return carry

    lax.fori_loop(1, n_blk, bias_send_one, 0)

    def summed(h):
        total = jnp.zeros((rows, width), jnp.float32)
        for r in range(n_rep):
            slot = h * n_rep + r

            def arrived():
                remote(
                    pbuf.at[0, 0], ghbuf.at[slot], bw_send.at[h, r], bw_recv.at[slot], me_b, me_r
                ).wait_recv()

            if r == 0:
                pl.when(me_r != 0)(arrived)
            else:
                arrived()
            total = total + ghbuf[slot].astype(jnp.float32)
        return total

    cross[...] = summed(1).astype(jnp.bfloat16)
    over = remote(cross, ghbuf.at[2 * n_rep], cross_send, cross_recv, partner, me_r)
    over.start()
    total = summed(0)
    over.wait_recv()
    total = total + ghbuf[2 * n_rep].astype(jnp.float32)
    gh = total.astype(jnp.bfloat16)
    w_terms = jnp.dot(feats_t[...], gh, preferred_element_type=jnp.float32).astype(jnp.bfloat16)
    for h in range(halves):
        terms[h] = w_terms[:, h * HALF:(h + 1) * HALF]

    def chunk_of(b, r):
        return terms.at[lax.rem(b, halves), pl.ds(pl.multiple_of(r * w_rows + b // halves * CHUNK, CHUNK), CHUNK)]

    def w_send_one(d, carry):
        other = lax.rem(me + d, n_dev)
        b, r = other // n_rep, lax.rem(other, n_rep)

        def go():
            remote(chunk_of(b, r), wbuf.at[n_dev - 1 - d], w_send, w_recv, b, r).start()

        if owners == n_blk:
            go()
        else:
            pl.when(b < owners)(go)
        return carry

    lax.fori_loop(1, n_dev, w_send_one, 0)
    gf_ref[...] = lax.dot_general(
        gh, weight_ref[...], (((1,), (1,)), ((), ())), preferred_element_type=jnp.float32
    ).astype(jnp.bfloat16)
    all_bias = bias_buf
    remote(all_bias, all_bias, bias_send, bias_recv, me_b, me_r).wait_recv()
    gb_ref[...] = (bias_mine[...] + jnp.sum(bias_buf[...], axis=0))[0:1]

    def fin_copy(d):
        to = lax.rem(me_b + d, n_blk)
        return remote(wsum, fin.at[me_b], fin_send.at[d], fin_recv.at[me_b], to, me_r)

    def own_chunk():
        remote(wbuf, wbuf, w_send, w_recv, me_b, me_r).wait_recv()
        mine = terms[
            lax.rem(me_b, halves), pl.ds(pl.multiple_of(me_r * w_rows + me_b // halves * CHUNK, CHUNK), CHUNK)
        ]
        wsum[...] = mine.astype(jnp.float32) + jnp.sum(wbuf[...].astype(jnp.float32), axis=0)
        for d in range(1, n_blk):
            fin_copy(d).start()
        fin[me_b] = wsum[...]

    if owners == n_blk:
        own_chunk()
    else:
        pl.when(me_b < owners)(own_chunk)
    for o in range(owners):
        @pl.when(me_b != o)
        def _():
            remote(wsum, fin.at[o], fin_send.at[0], fin_recv.at[o], me_b, me_r).wait_recv()

        at = o // halves * CHUNK
        gw_ref[at:at + CHUNK, (o % halves) * HALF:(o % halves + 1) * HALF] = fin[o]

    swap.wait_send()
    over.wait_send()
    for k in range(n_slot):
        for r in range(n_rep):
            if r == 0:
                @pl.when(me_r != 0)
                def _():
                    hw_copy(k, 0).wait_send()
                    bw_copy(k, 0).wait_send()
            else:
                hw_copy(k, r).wait_send()
                bw_copy(k, r).wait_send()
    for j in range(n_rep):
        @pl.when(me_r != j)
        def _():
            rs_copy(j).wait_send()
    for d in range(1, n_rep):
        ag_copy(d).wait_send()
    remote(all_bias, all_bias, bias_send, bias_recv, me_b, me_r).wait_send()
    if owners == n_blk:
        remote(wbuf, wbuf, w_send, w_recv, me_b, me_r).wait_send()
    else:
        def w_left(d, carry):
            other = lax.rem(me + d, n_dev)

            @pl.when(other // n_rep < owners)
            def _():
                remote(wbuf.at[0], wbuf.at[0], w_send, w_recv, me_b, me_r).wait_send()
            return carry

        lax.fori_loop(1, n_dev, w_left, 0)

    def fin_left():
        for d in range(1, n_blk):
            fin_copy(d).wait_send()

    if owners == n_blk:
        fin_left()
    else:
        pl.when(me_b < owners)(fin_left)


def body(feats, weight, bias, grad_out, tile_values, tile_rows, tile_cols, tile_count):
    n_blk = lax.axis_size("blk")
    n_rep = lax.axis_size("rep")
    n_slot, cells, tile = tile_values.shape[2:5]
    rows, width = feats.shape
    n_dev = n_blk * n_rep
    part_rows = rows * n_rep
    side = part_rows // tile
    w_rows = width // n_rep
    owners = (w_rows // CHUNK) * (width // HALF)

    named = tile_rows[0, 0] * side + tile_cols[0, 0]
    live = jnp.arange(cells, dtype=jnp.int32)[None] < tile_count[0, 0][:, None]
    entry = jnp.arange(n_slot * cells, dtype=jnp.int32).reshape(n_slot, cells)
    hit = (named[:, None, :] == jnp.arange(side * side, dtype=jnp.int32)[None, :, None]) & live[:, None, :]
    inv = jnp.min(jnp.where(hit, entry[:, None, :], n_slot * cells), axis=2).reshape(-1)

    assert n_slot == 2 and n_blk == 2 * n_rep
    bf16, f32 = jnp.bfloat16, jnp.float32
    vmem = pl.BlockSpec(memory_space=pltpu.VMEM)
    dma = pltpu.SemaphoreType.DMA
    out, gf, gw, gb = pl.pallas_call(
        functools.partial(layer_kernel, n_blk, n_rep, n_slot, tile, cells, side),
        out_shape=(
            jax.ShapeDtypeStruct((rows, width), bf16),
            jax.ShapeDtypeStruct((rows, width), bf16),
            jax.ShapeDtypeStruct((w_rows, width), f32),
            jax.ShapeDtypeStruct((1, width), f32),
        ),
        in_specs=[pl.BlockSpec(memory_space=pltpu.SMEM)] + [pl.BlockSpec(memory_space=pl.ANY)] * 5,
        out_specs=(vmem, vmem, vmem, vmem),
        scratch_shapes=[
            pltpu.VMEM((rows, width), bf16),
            pltpu.VMEM((width, width), bf16),
            pltpu.VMEM((1, width), f32),
            pltpu.VMEM((rows, width), bf16),
            pltpu.VMEM((n_slot * cells + 1, tile, tile), bf16),
            pltpu.VMEM((n_slot, part_rows, part_rows), bf16),
            pltpu.VMEM((rows, width), bf16),
            pltpu.VMEM((rows, width), bf16),
            pltpu.VMEM((n_slot, n_rep, rows, width), bf16),
            pltpu.VMEM((part_rows, width), f32),
            pltpu.VMEM((n_rep, rows, width), bf16),
            pltpu.VMEM((n_rep, rows, width), bf16),
            pltpu.VMEM((n_rep, rows, width), bf16),
            pltpu.VMEM((width, part_rows), bf16),
            pltpu.VMEM((n_slot, n_rep, rows, width), bf16),
            pltpu.VMEM((n_slot * n_rep + 1, rows, width), bf16),
            pltpu.VMEM((width, rows), bf16),
            pltpu.VMEM((rows, width), bf16),
            pltpu.VMEM((8, width), f32),
            pltpu.VMEM((n_blk - 1, 8, width), f32),
            pltpu.VMEM((width // HALF, width, HALF), bf16),
            pltpu.VMEM((n_dev - 1, CHUNK, HALF), bf16),
            pltpu.VMEM((CHUNK, HALF), f32),
            pltpu.VMEM((owners, CHUNK, HALF), f32),
            dma((4,)),
            dma((n_slot,)),
            dma,
            dma,
            dma,
            dma,
            dma((n_slot, n_rep)),
            dma((n_slot, n_rep)),
            dma((n_rep,)),
            dma((n_rep,)),
            dma((n_rep,)),
            dma((n_rep,)),
            dma((n_slot, n_rep)),
            dma((n_slot * n_rep,)),
            dma,
            dma,
            dma,
            dma,
            dma((n_blk,)),
            dma((owners,)),
        ],
        compiler_params=pltpu.CompilerParams(
            collective_id=0, has_side_effects=True, vmem_limit_bytes=56 * 2 ** 20
        ),
        name="graph_layer",
    )(inv, feats, weight, bias.reshape(1, width), grad_out, tile_values.reshape(n_slot * cells, tile, tile))
    return (out, gf, gw, gb.reshape(width))


def solution(mesh):
    in_specs = (
        P(("blk", "rep"), None),
        P(),
        P(),
        P(("blk", "rep"), None),
        P("blk", "rep", None, None, None, None),
        P("blk", "rep", None, None),
        P("blk", "rep", None, None),
        P("blk", "rep", None),
    )
    out_specs = (P(("blk", "rep"), None), P(("blk", "rep"), None), P("rep", None), P())
    return jax.shard_map(body, mesh=mesh, in_specs=in_specs, out_specs=out_specs, check_vma=False)
```

```python
import functools

import jax
import jax.numpy as jnp
from jax import lax
from jax.experimental import pallas as pl
from jax.experimental.pallas import tpu as pltpu
from jax.sharding import PartitionSpec as P

MESH = pl.DeviceIdType.MESH
UNIT = 256
CHUNK = 16
HALF = 128


def remote(src, dst, send, recv, blk, rep):
    return pltpu.make_async_remote_copy(
        src_ref=src, dst_ref=dst, send_sem=send, recv_sem=recv, device_id=(blk, rep), device_id_type=MESH
    )


def layer_kernel(
    n_blk, n_rep, n_slot, tile, cells, tiles_side,
    inv_ref, feats_hbm, weight_hbm, bias_hbm, gout_hbm, tiles_hbm,
    out_hbm, gf_hbm, gw_hbm, gb_hbm,
    feats_ref, weight_ref, bias_ref, gout_ref, out_ref, gf_ref, gw_ref, gb_ref,
    tiles, dense, dense_t, hw, hw_other, hwbuf, acc, part, aggbuf, gbuf, pbuf, ghbuf, feats_t,
    cross, bias_mine, bias_buf, terms, wbuf, wsum, fin,
    in_sem, out_sem, tile_sem, swap_send, swap_recv, cross_send, cross_recv, hw_send, hw_recv,
    rs_send, rs_recv, ag_send, ag_recv, bw_send, bw_recv,
    bias_send, bias_recv, w_send, w_recv, fin_send, fin_recv,
):
    n_dev = n_blk * n_rep
    rows, width = feats_ref.shape
    units = rows * n_rep // UNIT
    per = UNIT // rows
    w_rows = width // n_rep
    halves = width // HALF
    groups = w_rows // CHUNK
    owners = groups * halves
    f32, bf16 = jnp.float32, jnp.bfloat16
    me_b = lax.axis_index("blk")
    me_r = lax.axis_index("rep")
    me = me_b * n_rep + me_r
    half = me_b // n_rep
    place = lax.rem(me_b, n_rep)
    partner = lax.rem(me_b + n_rep, n_blk)
    near_slot = jnp.where(place < me_r, 1, 0)

    def columns(c):
        return slice(c * HALF, (c + 1) * HALF)

    def unless(i, task):
        if i == 0:
            pl.when(me_r != 0)(task)
        else:
            task()

    small = []
    for i, (src, dst) in enumerate(
        ((feats_hbm, feats_ref), (weight_hbm, weight_ref), (bias_hbm, bias_ref), (gout_hbm, gout_ref))
    ):
        small.append(pltpu.make_async_copy(src, dst, in_sem.at[i]))
        small[-1].start()
    loads = []
    for k in range(n_slot):
        span = pl.ds(k * cells, cells)
        load = pltpu.make_async_copy(tiles_hbm.at[span], tiles.at[span], tile_sem.at[k])
        load.start()
        loads.append(load)
    barrier = pltpu.get_barrier_semaphore()

    def greet(d, carry):
        other = lax.rem(me + d, n_dev)
        pl.semaphore_signal(
            barrier, inc=1, device_id=(other // n_rep, lax.rem(other, n_rep)), device_id_type=MESH
        )
        return carry

    lax.fori_loop(1, n_dev, greet, 0)

    small[0].wait()
    small[1].wait()
    first = jnp.dot(feats_ref[...], weight_ref[...], preferred_element_type=f32).astype(bf16)
    for c in range(halves):
        hw[c] = first[:, columns(c)]
    pl.semaphore_wait(barrier, n_dev - 1)

    swaps = [
        remote(hw.at[c], hw_other.at[c], swap_send.at[c], swap_recv.at[c], partner, me_r) for c in range(halves)
    ]

    def hw_copy(c, h, r):
        to = half * n_rep + lax.rem(place + r, n_rep)
        src = hw if h == 0 else hw_other
        return remote(src.at[c], hwbuf.at[c, h, me_r], hw_send.at[c, h, r], hw_recv.at[c, h, me_r], to, r)

    def hw_share(c, h):
        for r in reversed(range(n_rep)):
            unless(r, lambda: hw_copy(c, h, r).start())

        @pl.when(me_r == 0)
        def _():
            hwbuf[c, h, 0] = hw[c] if h == 0 else hw_other[c]

    def fill(h):
        base = jnp.where(near_slot == 1, 1 - h, h) * tiles_side * tiles_side

        def fill_rows(r, carry):
            at = pl.ds(pl.multiple_of(r * tile, tile), tile)
            for c in range(tiles_side):
                dense[h, at, c * tile:(c + 1) * tile] = tiles[inv_ref[base + r * tiles_side + c]]
            return carry

        lax.fori_loop(0, tiles_side, fill_rows, 0)

    def fill_transposed(h):
        base = jnp.where(near_slot == 1, 1 - h, h) * tiles_side * tiles_side

        def fill_rows(c, carry):
            at = pl.ds(pl.multiple_of(c * tile, tile), tile)
            for r in range(tiles_side):
                dense_t[h, at, r * tile:(r + 1) * tile] = tiles[inv_ref[base + r * tiles_side + c]].T
            return carry

        lax.fori_loop(0, tiles_side, fill_rows, 0)

    for c in range(halves):
        swaps[c].start()
        if c == 0:
            hw_share(0, 0)
    tiles[n_slot * cells] = jnp.zeros((tile, tile), bf16)
    for load in loads:
        load.wait()
    fill(0)
    swaps[0].wait_recv()
    hw_share(0, 1)
    for c in range(1, halves):
        hw_share(c, 0)
    fill(1)
    for c in range(1, halves):
        swaps[c].wait_recv()
        hw_share(c, 1)
    fill_transposed(1)
    fill_transposed(0)
    feats_t[...] = feats_ref[...].T

    def hw_wait(c, h, src):
        remote(
            hw.at[c], hwbuf.at[c, h, src], hw_send.at[c, h, src], hw_recv.at[c, h, src], me_b, me_r
        ).wait_recv()

    def rs_copy(c, j):
        return remote(part.at[c, j], aggbuf.at[c, me_r], rs_send.at[c, j], rs_recv.at[c, me_r], me_b, j)

    def forward(c):
        for h in range(2):
            for u in range(units):
                for src in range(u * per, (u + 1) * per):
                    unless(src, lambda: hw_wait(c, h, src))
                rhs = hwbuf[c, h, u * per:(u + 1) * per].reshape(UNIT, HALF)
                last = h == 1 and u == units - 1
                for j in range(units):
                    at = slice(j * UNIT, (j + 1) * UNIT)
                    got = jnp.dot(dense[h, at, u * UNIT:(u + 1) * UNIT], rhs, preferred_element_type=f32)
                    if h + u > 0:
                        got = got + acc[c, at]
                    acc[c, at] = got
                    if last:
                        part[c, j * per:(j + 1) * per] = got.astype(bf16).reshape(per, rows, HALF)
                        for i in range(j * per, (j + 1) * per):
                            pl.when(me_r != i)(lambda: rs_copy(c, i).start())

    def ag_copy(c, d):
        to = lax.rem(me_r + d, n_rep)
        return remote(
            gbuf.at[c, me_r], gbuf.at[c, me_r], ag_send.at[c, d], ag_recv.at[c, me_r], me_b, to
        )

    def activate(c):
        total = acc[c, pl.ds(pl.multiple_of(me_r * rows, rows), rows)]
        for d in range(1, n_rep):
            src = lax.rem(me_r + d, n_rep)
            remote(
                part.at[c, 0], aggbuf.at[c, src], rs_send.at[c, src], rs_recv.at[c, src], me_b, src
            ).wait_recv()
            total = total + aggbuf[c, src].astype(f32)
        pre = total + bias_ref[:, columns(c)]
        logistic = jax.nn.sigmoid(pre)
        cotangent = gout_ref[:, columns(c)].astype(f32)
        gbuf[c, me_r] = (cotangent * logistic * (1.0 + pre * (1.0 - logistic))).astype(bf16)
        for d in range(1, n_rep):
            ag_copy(c, d).start()
        out_ref[:, columns(c)] = (pre * logistic).astype(bf16)

    def bw_copy(c, h, j):
        to = half * n_rep + lax.rem(place - me_r + n_rep, n_rep)
        slot = h * n_rep + me_r
        return remote(pbuf.at[c, h, j], ghbuf.at[c, slot], bw_send.at[c, h, j], bw_recv.at[c, slot], to, j)

    def backward(c):
        for d in range(1, n_rep):
            src = lax.rem(me_r + d, n_rep)
            remote(
                gbuf.at[c, src], gbuf.at[c, src], ag_send.at[c, d], ag_recv.at[c, src], me_b, src
            ).wait_recv()
        grads = gbuf[c].reshape(rows * n_rep, HALF)
        for h in (1, 0):
            for u in range(units):
                term = jnp.dot(dense_t[h, u * UNIT:(u + 1) * UNIT], grads, preferred_element_type=f32)
                pbuf[c, h, u * per:(u + 1) * per] = term.astype(bf16).reshape(per, rows, HALF)
                for j in range(u * per, (u + 1) * per):
                    unless(j, lambda: bw_copy(c, h, j).start())
                    if j == 0:
                        @pl.when(me_r == 0)
                        def _():
                            ghbuf[c, h * n_rep] = pbuf[c, h, 0]
        bias_mine[:, columns(c)] = jnp.dot(
            jnp.ones((8, rows * n_rep), bf16), grads, preferred_element_type=f32
        )

    def arrived(c, slot):
        remote(
            pbuf.at[c, 0, 0], ghbuf.at[c, slot], bw_send.at[c, 0, 0], bw_recv.at[c, slot], me_b, me_r
        ).wait_recv()

    def summed(c, h):
        total = jnp.zeros((rows, HALF), f32)
        for r in range(n_rep):
            unless(r, lambda: arrived(c, h * n_rep + r))
            total = total + ghbuf[c, h * n_rep + r].astype(f32)
        return total

    overs = [
        remote(cross.at[c], ghbuf.at[c, 2 * n_rep], cross_send.at[c], cross_recv.at[c], partner, me_r)
        for c in range(halves)
    ]

    def send_over(c):
        cross[c] = summed(c, 1).astype(bf16)
        overs[c].start()

    def w_copy(c, g, r):
        to = (g * halves + c) * n_rep + r
        slot = lax.rem(me - to + n_dev, n_dev) - 1
        at = r * w_rows + g * CHUNK
        return remote(
            terms.at[c, at:at + CHUNK], wbuf.at[slot], w_send, w_recv, g * halves + c, r
        )

    def owned(c):
        total = summed(c, 0)
        overs[c].wait_recv()
        gh = (total + ghbuf[c, 2 * n_rep].astype(f32)).astype(bf16)
        terms[c] = jnp.dot(feats_t[...], gh, preferred_element_type=f32).astype(bf16)
        for g in range(groups):
            for r in range(n_rep):
                pl.when(me != (g * halves + c) * n_rep + r)(lambda: w_copy(c, g, r).start())
        return lax.dot_general(
            gh, weight_ref[:, columns(c)], (((1,), (1,)), ((), ())), preferred_element_type=f32
        )

    for c in range(halves):
        forward(c)
    small[2].wait()
    small[3].wait()
    for c in range(halves):
        activate(c)
    results = [
        pltpu.make_async_copy(src, dst, out_sem.at[i])
        for i, (src, dst) in enumerate(
            ((out_ref, out_hbm), (gf_ref, gf_hbm), (gw_ref, gw_hbm), (gb_ref, gb_hbm))
        )
    ]
    results[0].start()
    for c in range(halves):
        backward(c)

    def bias_send_one(d, carry):
        to = lax.rem(me_b + d, n_blk)
        remote(bias_mine, bias_buf.at[n_blk - 1 - d], bias_send, bias_recv, to, me_r).start()
        return carry

    lax.fori_loop(1, n_blk, bias_send_one, 0)

    for c in range(halves):
        send_over(c)
    feat_grad = owned(0)
    for c in range(1, halves):
        feat_grad = feat_grad + owned(c)
    gf_ref[...] = feat_grad.astype(bf16)
    results[1].start()
    remote(bias_buf, bias_buf, bias_send, bias_recv, me_b, me_r).wait_recv()
    gb_ref[...] = (bias_mine[...] + jnp.sum(bias_buf[...], axis=0))[0:1]
    results[3].start()

    def fin_copy(d):
        to = lax.rem(me_b + d, n_blk)
        return remote(wsum, fin.at[me_b], fin_send.at[d], fin_recv.at[me_b], to, me_r)

    def own_chunk():
        remote(wbuf, wbuf, w_send, w_recv, me_b, me_r).wait_recv()
        mine = terms[
            lax.rem(me_b, halves), pl.ds(pl.multiple_of(me_r * w_rows + me_b // halves * CHUNK, CHUNK), CHUNK)
        ]
        wsum[...] = mine.astype(f32) + jnp.sum(wbuf[...].astype(f32), axis=0)
        for d in range(1, n_blk):
            fin_copy(d).start()
        fin[me_b] = wsum[...]

    if owners == n_blk:
        own_chunk()
    else:
        pl.when(me_b < owners)(own_chunk)
    for o in range(owners):
        @pl.when(me_b != o)
        def _():
            remote(wsum, fin.at[o], fin_send.at[0], fin_recv.at[o], me_b, me_r).wait_recv()

        at = o // halves * CHUNK
        gw_ref[at:at + CHUNK, columns(o % halves)] = fin[o]
    results[2].start()

    for c in range(halves):
        swaps[c].wait_send()
        overs[c].wait_send()
        for h in range(2):
            for r in range(n_rep):
                unless(r, lambda: hw_copy(c, h, r).wait_send())
                unless(r, lambda: bw_copy(c, h, r).wait_send())
        for j in range(n_rep):
            pl.when(me_r != j)(lambda: rs_copy(c, j).wait_send())
        for d in range(1, n_rep):
            ag_copy(c, d).wait_send()
    remote(bias_buf, bias_buf, bias_send, bias_recv, me_b, me_r).wait_send()
    if owners == n_blk:
        remote(wbuf, wbuf, w_send, w_recv, me_b, me_r).wait_send()
    else:
        for c in range(halves):
            for g in range(groups):
                for r in range(n_rep):
                    pl.when(me != (g * halves + c) * n_rep + r)(lambda: w_copy(c, g, r).wait_send())

    def fin_left():
        for d in range(1, n_blk):
            fin_copy(d).wait_send()

    if owners == n_blk:
        fin_left()
    else:
        pl.when(me_b < owners)(fin_left)
    for result in results:
        result.wait()


def deliver_kernel(*refs):
    count = len(refs) // 2
    sems = refs[-1]
    copies = [pltpu.make_async_copy(refs[i], refs[count + i], sems.at[i]) for i in range(count)]
    for copy in copies:
        copy.start()
    for copy in copies:
        copy.wait()


def body(feats, weight, bias, grad_out, tile_values, tile_rows, tile_cols, tile_count):
    n_blk = lax.axis_size("blk")
    n_rep = lax.axis_size("rep")
    n_slot, cells, tile = tile_values.shape[2:5]
    rows, width = feats.shape
    n_dev = n_blk * n_rep
    part_rows = rows * n_rep
    side = part_rows // tile
    w_rows = width // n_rep
    owners = (w_rows // CHUNK) * (width // HALF)

    named = tile_rows[0, 0] * side + tile_cols[0, 0]
    live = jnp.arange(cells, dtype=jnp.int32)[None] < tile_count[0, 0][:, None]
    entry = jnp.arange(n_slot * cells, dtype=jnp.int32).reshape(n_slot, cells)
    hit = (named[:, None, :] == jnp.arange(side * side, dtype=jnp.int32)[None, :, None]) & live[:, None, :]
    inv = jnp.min(jnp.where(hit, entry[:, None, :], n_slot * cells), axis=2).reshape(-1)

    assert n_slot == 2 and n_blk == 2 * n_rep
    bf16, f32 = jnp.bfloat16, jnp.float32
    halves = width // HALF
    anywhere = pl.BlockSpec(memory_space=pl.ANY)
    dma = pltpu.SemaphoreType.DMA
    shapes = (
        jax.ShapeDtypeStruct((rows, width), bf16),
        jax.ShapeDtypeStruct((rows, width), bf16),
        jax.ShapeDtypeStruct((w_rows, width), f32),
        jax.ShapeDtypeStruct((1, width), f32),
    )
    results = pl.pallas_call(
        functools.partial(layer_kernel, n_blk, n_rep, n_slot, tile, cells, side),
        out_shape=shapes,
        in_specs=[pl.BlockSpec(memory_space=pltpu.SMEM)] + [anywhere] * 5,
        out_specs=(anywhere,) * 4,
        scratch_shapes=[
            pltpu.VMEM((rows, width), bf16),
            pltpu.VMEM((width, width), bf16),
            pltpu.VMEM((1, width), f32),
            pltpu.VMEM((rows, width), bf16),
            pltpu.VMEM((rows, width), bf16),
            pltpu.VMEM((rows, width), bf16),
            pltpu.VMEM((w_rows, width), f32),
            pltpu.VMEM((1, width), f32),
            pltpu.VMEM((n_slot * cells + 1, tile, tile), bf16),
            pltpu.VMEM((n_slot, part_rows, part_rows), bf16),
            pltpu.VMEM((n_slot, part_rows, part_rows), bf16),
            pltpu.VMEM((halves, rows, HALF), bf16),
            pltpu.VMEM((halves, rows, HALF), bf16),
            pltpu.VMEM((halves, n_slot, n_rep, rows, HALF), bf16),
            pltpu.VMEM((halves, part_rows, HALF), f32),
            pltpu.VMEM((halves, n_rep, rows, HALF), bf16),
            pltpu.VMEM((halves, n_rep, rows, HALF), bf16),
            pltpu.VMEM((halves, n_rep, rows, HALF), bf16),
            pltpu.VMEM((halves, n_slot, n_rep, rows, HALF), bf16),
            pltpu.VMEM((halves, n_slot * n_rep + 1, rows, HALF), bf16),
            pltpu.VMEM((width, rows), bf16),
            pltpu.VMEM((halves, rows, HALF), bf16),
            pltpu.VMEM((8, width), f32),
            pltpu.VMEM((n_blk - 1, 8, width), f32),
            pltpu.VMEM((halves, width, HALF), bf16),
            pltpu.VMEM((n_dev - 1, CHUNK, HALF), bf16),
            pltpu.VMEM((CHUNK, HALF), f32),
            pltpu.VMEM((owners, CHUNK, HALF), f32),
            dma((4,)),
            dma((4,)),
            dma((n_slot,)),
            dma((halves,)),
            dma((halves,)),
            dma((halves,)),
            dma((halves,)),
            dma((halves, n_slot, n_rep)),
            dma((halves, n_slot, n_rep)),
            dma((halves, n_rep)),
            dma((halves, n_rep)),
            dma((halves, n_rep)),
            dma((halves, n_rep)),
            dma((halves, n_slot, n_rep)),
            dma((halves, n_slot * n_rep)),
            dma,
            dma,
            dma,
            dma,
            dma((n_blk,)),
            dma((owners,)),
        ],
        compiler_params=pltpu.CompilerParams(
            collective_id=0, has_side_effects=True, vmem_limit_bytes=56 * 2 ** 20
        ),
        name="graph_layer",
    )(inv, feats, weight, bias.reshape(1, width), grad_out, tile_values.reshape(n_slot * cells, tile, tile))
    out, gf, gw, gb = pl.pallas_call(
        deliver_kernel,
        out_shape=shapes,
        in_specs=[anywhere] * 4,
        out_specs=(anywhere,) * 4,
        scratch_shapes=[dma((4,))],
        name="deliver",
    )(*results)
    return (out, gf, gw, gb.reshape(width))


def solution(mesh):
    in_specs = (
        P(("blk", "rep"), None),
        P(),
        P(),
        P(("blk", "rep"), None),
        P("blk", "rep", None, None, None, None),
        P("blk", "rep", None, None),
        P("blk", "rep", None, None),
        P("blk", "rep", None),
    )
    out_specs = (P(("blk", "rep"), None), P(("blk", "rep"), None), P("rep", None), P())
    return jax.shard_map(body, mesh=mesh, in_specs=in_specs, out_specs=out_specs, check_vma=False)
```

```python
import functools

import jax
import jax.numpy as jnp
from jax import lax
from jax.experimental import pallas as pl
from jax.experimental.pallas import tpu as pltpu
from jax.sharding import PartitionSpec as P

MESH = pl.DeviceIdType.MESH
UNIT = 256
CHUNK = 16
HALF = 128


def remote(src, dst, send, recv, blk, rep):
    return pltpu.make_async_remote_copy(
        src_ref=src, dst_ref=dst, send_sem=send, recv_sem=recv, device_id=(blk, rep), device_id_type=MESH
    )


def layer_kernel(
    n_blk, n_rep, n_slot, tile, cells, tiles_side,
    inv_ref, feats_hbm, weight_hbm, bias_hbm, gout_hbm, tiles_hbm,
    out_hbm, gf_hbm, gw_hbm, gb_hbm,
    feats_ref, weight_ref, bias_ref, gout_ref, out_ref, gf_ref, gw_ref, gb_ref,
    tiles, dense, dense_t, hw, hw_other, hwbuf, acc, part, aggbuf, gbuf, pbuf, ghbuf, feats_t,
    cross, bias_mine, bias_buf, terms, wbuf, wsum, fin,
    in_sem, out_sem, tile_sem, swap_send, swap_recv, cross_send, cross_recv, hw_send, hw_recv,
    rs_send, rs_recv, ag_send, ag_recv, bw_send, bw_recv,
    bias_send, bias_recv, w_send, w_recv, fin_send, fin_recv,
):
    n_dev = n_blk * n_rep
    rows, width = feats_ref.shape
    units = rows * n_rep // UNIT
    per = UNIT // rows
    w_rows = width // n_rep
    halves = width // HALF
    groups = w_rows // CHUNK
    owners = groups * halves
    f32, bf16 = jnp.float32, jnp.bfloat16
    me_b = lax.axis_index("blk")
    me_r = lax.axis_index("rep")
    me = me_b * n_rep + me_r
    half = me_b // n_rep
    place = lax.rem(me_b, n_rep)
    partner = lax.rem(me_b + n_rep, n_blk)
    near_slot = jnp.where(place < me_r, 1, 0)

    def columns(c):
        return slice(c * HALF, (c + 1) * HALF)

    def unless(i, task):
        if i == 0:
            pl.when(me_r != 0)(task)
        else:
            task()

    small = []
    for i, (src, dst) in enumerate(
        ((feats_hbm, feats_ref), (weight_hbm, weight_ref), (bias_hbm, bias_ref), (gout_hbm, gout_ref))
    ):
        small.append(pltpu.make_async_copy(src, dst, in_sem.at[i]))
        small[-1].start()
    loads = []
    for k in range(n_slot):
        span = pl.ds(k * cells, cells)
        load = pltpu.make_async_copy(tiles_hbm.at[span], tiles.at[span], tile_sem.at[k])
        load.start()
        loads.append(load)
    barrier = pltpu.get_barrier_semaphore()

    def greet(d, carry):
        other = lax.rem(me + d, n_dev)
        pl.semaphore_signal(
            barrier, inc=1, device_id=(other // n_rep, lax.rem(other, n_rep)), device_id_type=MESH
        )
        return carry

    lax.fori_loop(1, n_dev, greet, 0)

    small[0].wait()
    small[1].wait()
    first = jnp.dot(feats_ref[...], weight_ref[...], preferred_element_type=f32).astype(bf16)
    for c in range(halves):
        hw[c] = first[:, columns(c)]
    pl.semaphore_wait(barrier, n_dev - 1)

    swaps = [
        remote(hw.at[c], hw_other.at[c], swap_send.at[c], swap_recv.at[c], partner, me_r) for c in range(halves)
    ]

    def hw_copy(c, h, r):
        to = half * n_rep + lax.rem(place + r, n_rep)
        src = hw if h == 0 else hw_other
        return remote(src.at[c], hwbuf.at[c, h, me_r], hw_send.at[c, h, r], hw_recv.at[c, h, me_r], to, r)

    def hw_share(c, h):
        for r in reversed(range(n_rep)):
            unless(r, lambda: hw_copy(c, h, r).start())

        @pl.when(me_r == 0)
        def _():
            hwbuf[c, h, 0] = hw[c] if h == 0 else hw_other[c]

    def fill(h):
        base = jnp.where(near_slot == 1, 1 - h, h) * tiles_side * tiles_side

        def fill_rows(r, carry):
            at = pl.ds(pl.multiple_of(r * tile, tile), tile)
            for c in range(tiles_side):
                dense[h, at, c * tile:(c + 1) * tile] = tiles[inv_ref[base + r * tiles_side + c]]
            return carry

        lax.fori_loop(0, tiles_side, fill_rows, 0)

    def fill_transposed(h):
        base = jnp.where(near_slot == 1, 1 - h, h) * tiles_side * tiles_side

        def fill_rows(c, carry):
            at = pl.ds(pl.multiple_of(c * tile, tile), tile)
            for r in range(tiles_side):
                dense_t[h, at, r * tile:(r + 1) * tile] = tiles[inv_ref[base + r * tiles_side + c]].T
            return carry

        lax.fori_loop(0, tiles_side, fill_rows, 0)

    for c in range(halves):
        swaps[c].start()
        if c == 0:
            hw_share(0, 0)
    tiles[n_slot * cells] = jnp.zeros((tile, tile), bf16)
    for load in loads:
        load.wait()
    fill(0)
    swaps[0].wait_recv()
    hw_share(0, 1)
    for c in range(1, halves):
        hw_share(c, 0)
    fill(1)
    for c in range(1, halves):
        swaps[c].wait_recv()
        hw_share(c, 1)
    fill_transposed(1)
    fill_transposed(0)
    feats_t[...] = feats_ref[...].T

    def hw_wait(c, h, src):
        remote(
            hw.at[c], hwbuf.at[c, h, src], hw_send.at[c, h, src], hw_recv.at[c, h, src], me_b, me_r
        ).wait_recv()

    def rs_copy(c, j):
        return remote(part.at[c, j], aggbuf.at[c, me_r], rs_send.at[c, j], rs_recv.at[c, me_r], me_b, j)

    def forward(c):
        for h in range(2):
            for src in range(n_rep):
                unless(src, lambda: hw_wait(c, h, src))
            source = hwbuf[c, h].reshape(rows * n_rep, HALF)
            for j in range(units):
                at = slice(j * UNIT, (j + 1) * UNIT)
                got = jnp.dot(dense[h, at], source, preferred_element_type=f32)
                if h == 0:
                    acc[c, at] = got
                else:
                    got = got + acc[c, at]
                    acc[c, at] = got
                    part[c, j * per:(j + 1) * per] = got.astype(bf16).reshape(per, rows, HALF)
                    for i in range(j * per, (j + 1) * per):
                        pl.when(me_r != i)(lambda: rs_copy(c, i).start())

    def ag_copy(c, d):
        to = lax.rem(me_r + d, n_rep)
        return remote(
            gbuf.at[c, me_r], gbuf.at[c, me_r], ag_send.at[c, d], ag_recv.at[c, me_r], me_b, to
        )

    def activate(c):
        total = acc[c, pl.ds(pl.multiple_of(me_r * rows, rows), rows)]
        for d in range(1, n_rep):
            src = lax.rem(me_r + d, n_rep)
            remote(
                part.at[c, 0], aggbuf.at[c, src], rs_send.at[c, src], rs_recv.at[c, src], me_b, src
            ).wait_recv()
            total = total + aggbuf[c, src].astype(f32)
        pre = total + bias_ref[:, columns(c)]
        logistic = jax.nn.sigmoid(pre)
        cotangent = gout_ref[:, columns(c)].astype(f32)
        gbuf[c, me_r] = (cotangent * logistic * (1.0 + pre * (1.0 - logistic))).astype(bf16)
        for d in range(1, n_rep):
            ag_copy(c, d).start()
        out_ref[:, columns(c)] = (pre * logistic).astype(bf16)

    def bw_copy(c, h, j):
        to = half * n_rep + lax.rem(place - me_r + n_rep, n_rep)
        slot = h * n_rep + me_r
        return remote(pbuf.at[c, h, j], ghbuf.at[c, slot], bw_send.at[c, h, j], bw_recv.at[c, slot], to, j)

    def backward(c):
        for d in range(1, n_rep):
            src = lax.rem(me_r + d, n_rep)
            remote(
                gbuf.at[c, src], gbuf.at[c, src], ag_send.at[c, d], ag_recv.at[c, src], me_b, src
            ).wait_recv()
        grads = gbuf[c].reshape(rows * n_rep, HALF)
        for h in (1, 0):
            for u in range(units):
                term = jnp.dot(dense_t[h, u * UNIT:(u + 1) * UNIT], grads, preferred_element_type=f32)
                pbuf[c, h, u * per:(u + 1) * per] = term.astype(bf16).reshape(per, rows, HALF)
                for j in range(u * per, (u + 1) * per):
                    unless(j, lambda: bw_copy(c, h, j).start())
                    if j == 0:
                        @pl.when(me_r == 0)
                        def _():
                            ghbuf[c, h * n_rep] = pbuf[c, h, 0]
        bias_mine[:, columns(c)] = jnp.dot(
            jnp.ones((8, rows * n_rep), bf16), grads, preferred_element_type=f32
        )

    def arrived(c, slot):
        remote(
            pbuf.at[c, 0, 0], ghbuf.at[c, slot], bw_send.at[c, 0, 0], bw_recv.at[c, slot], me_b, me_r
        ).wait_recv()

    def summed(c, h):
        total = jnp.zeros((rows, HALF), f32)
        for r in range(n_rep):
            unless(r, lambda: arrived(c, h * n_rep + r))
            total = total + ghbuf[c, h * n_rep + r].astype(f32)
        return total

    overs = [
        remote(cross.at[c], ghbuf.at[c, 2 * n_rep], cross_send.at[c], cross_recv.at[c], partner, me_r)
        for c in range(halves)
    ]

    def send_over(c):
        cross[c] = summed(c, 1).astype(bf16)
        overs[c].start()

    def w_copy(c, g, r):
        to = (g * halves + c) * n_rep + r
        slot = lax.rem(me - to + n_dev, n_dev) - 1
        at = r * w_rows + g * CHUNK
        return remote(
            terms.at[c, at:at + CHUNK], wbuf.at[slot], w_send, w_recv, g * halves + c, r
        )

    def owned(c):
        total = summed(c, 0)
        overs[c].wait_recv()
        gh = (total + ghbuf[c, 2 * n_rep].astype(f32)).astype(bf16)
        terms[c] = jnp.dot(feats_t[...], gh, preferred_element_type=f32).astype(bf16)
        for g in range(groups):
            for r in range(n_rep):
                pl.when(me != (g * halves + c) * n_rep + r)(lambda: w_copy(c, g, r).start())
        return lax.dot_general(
            gh, weight_ref[:, columns(c)], (((1,), (1,)), ((), ())), preferred_element_type=f32
        )

    for c in range(halves):
        forward(c)
    small[2].wait()
    small[3].wait()
    for c in range(halves):
        activate(c)
    results = [
        pltpu.make_async_copy(src, dst, out_sem.at[i])
        for i, (src, dst) in enumerate(
            ((out_ref, out_hbm), (gf_ref, gf_hbm), (gw_ref, gw_hbm), (gb_ref, gb_hbm))
        )
    ]
    results[0].start()
    for c in range(halves):
        backward(c)

    def bias_send_one(d, carry):
        to = lax.rem(me_b + d, n_blk)
        remote(bias_mine, bias_buf.at[n_blk - 1 - d], bias_send, bias_recv, to, me_r).start()
        return carry

    lax.fori_loop(1, n_blk, bias_send_one, 0)

    for c in range(halves):
        send_over(c)
    feat_grad = owned(0)
    for c in range(1, halves):
        feat_grad = feat_grad + owned(c)
    gf_ref[...] = feat_grad.astype(bf16)
    results[1].start()
    remote(bias_buf, bias_buf, bias_send, bias_recv, me_b, me_r).wait_recv()
    gb_ref[...] = (bias_mine[...] + jnp.sum(bias_buf[...], axis=0))[0:1]
    results[3].start()

    def fin_copy(d):
        to = lax.rem(me_b + d, n_blk)
        return remote(wsum, fin.at[me_b], fin_send.at[d], fin_recv.at[me_b], to, me_r)

    def own_chunk():
        remote(wbuf, wbuf, w_send, w_recv, me_b, me_r).wait_recv()
        mine = terms[
            lax.rem(me_b, halves), pl.ds(pl.multiple_of(me_r * w_rows + me_b // halves * CHUNK, CHUNK), CHUNK)
        ]
        wsum[...] = mine.astype(f32) + jnp.sum(wbuf[...].astype(f32), axis=0)
        for d in range(1, n_blk):
            fin_copy(d).start()
        fin[me_b] = wsum[...]

    if owners == n_blk:
        own_chunk()
    else:
        pl.when(me_b < owners)(own_chunk)
    for o in range(owners):
        @pl.when(me_b != o)
        def _():
            remote(wsum, fin.at[o], fin_send.at[0], fin_recv.at[o], me_b, me_r).wait_recv()

        at = o // halves * CHUNK
        gw_ref[at:at + CHUNK, columns(o % halves)] = fin[o]
    results[2].start()

    for c in range(halves):
        swaps[c].wait_send()
        overs[c].wait_send()
        for h in range(2):
            for r in range(n_rep):
                unless(r, lambda: hw_copy(c, h, r).wait_send())
                unless(r, lambda: bw_copy(c, h, r).wait_send())
        for j in range(n_rep):
            pl.when(me_r != j)(lambda: rs_copy(c, j).wait_send())
        for d in range(1, n_rep):
            ag_copy(c, d).wait_send()
    remote(bias_buf, bias_buf, bias_send, bias_recv, me_b, me_r).wait_send()
    if owners == n_blk:
        remote(wbuf, wbuf, w_send, w_recv, me_b, me_r).wait_send()
    else:
        for c in range(halves):
            for g in range(groups):
                for r in range(n_rep):
                    pl.when(me != (g * halves + c) * n_rep + r)(lambda: w_copy(c, g, r).wait_send())

    def fin_left():
        for d in range(1, n_blk):
            fin_copy(d).wait_send()

    if owners == n_blk:
        fin_left()
    else:
        pl.when(me_b < owners)(fin_left)
    for result in results:
        result.wait()


def deliver_kernel(*refs):
    count = len(refs) // 2
    for src, dst in zip(refs[:count], refs[count:]):
        dst[...] = src[...]


def body(feats, weight, bias, grad_out, tile_values, tile_rows, tile_cols, tile_count):
    n_blk = lax.axis_size("blk")
    n_rep = lax.axis_size("rep")
    n_slot, cells, tile = tile_values.shape[2:5]
    rows, width = feats.shape
    n_dev = n_blk * n_rep
    part_rows = rows * n_rep
    side = part_rows // tile
    w_rows = width // n_rep
    owners = (w_rows // CHUNK) * (width // HALF)

    named = tile_rows[0, 0] * side + tile_cols[0, 0]
    live = jnp.arange(cells, dtype=jnp.int32)[None] < tile_count[0, 0][:, None]
    entry = jnp.arange(n_slot * cells, dtype=jnp.int32).reshape(n_slot, cells)
    hit = (named[:, None, :] == jnp.arange(side * side, dtype=jnp.int32)[None, :, None]) & live[:, None, :]
    inv = jnp.min(jnp.where(hit, entry[:, None, :], n_slot * cells), axis=2).reshape(-1)

    assert n_slot == 2 and n_blk == 2 * n_rep
    bf16, f32 = jnp.bfloat16, jnp.float32
    halves = width // HALF
    vmem = pl.BlockSpec(memory_space=pltpu.VMEM)
    anywhere = pl.BlockSpec(memory_space=pl.ANY)
    dma = pltpu.SemaphoreType.DMA
    shapes = (
        jax.ShapeDtypeStruct((rows, width), bf16),
        jax.ShapeDtypeStruct((rows, width), bf16),
        jax.ShapeDtypeStruct((w_rows, width), f32),
        jax.ShapeDtypeStruct((1, width), f32),
    )
    results = pl.pallas_call(
        functools.partial(layer_kernel, n_blk, n_rep, n_slot, tile, cells, side),
        out_shape=shapes,
        in_specs=[pl.BlockSpec(memory_space=pltpu.SMEM)] + [anywhere] * 5,
        out_specs=(anywhere,) * 4,
        scratch_shapes=[
            pltpu.VMEM((rows, width), bf16),
            pltpu.VMEM((width, width), bf16),
            pltpu.VMEM((1, width), f32),
            pltpu.VMEM((rows, width), bf16),
            pltpu.VMEM((rows, width), bf16),
            pltpu.VMEM((rows, width), bf16),
            pltpu.VMEM((w_rows, width), f32),
            pltpu.VMEM((1, width), f32),
            pltpu.VMEM((n_slot * cells + 1, tile, tile), bf16),
            pltpu.VMEM((n_slot, part_rows, part_rows), bf16),
            pltpu.VMEM((n_slot, part_rows, part_rows), bf16),
            pltpu.VMEM((halves, rows, HALF), bf16),
            pltpu.VMEM((halves, rows, HALF), bf16),
            pltpu.VMEM((halves, n_slot, n_rep, rows, HALF), bf16),
            pltpu.VMEM((halves, part_rows, HALF), f32),
            pltpu.VMEM((halves, n_rep, rows, HALF), bf16),
            pltpu.VMEM((halves, n_rep, rows, HALF), bf16),
            pltpu.VMEM((halves, n_rep, rows, HALF), bf16),
            pltpu.VMEM((halves, n_slot, n_rep, rows, HALF), bf16),
            pltpu.VMEM((halves, n_slot * n_rep + 1, rows, HALF), bf16),
            pltpu.VMEM((width, rows), bf16),
            pltpu.VMEM((halves, rows, HALF), bf16),
            pltpu.VMEM((8, width), f32),
            pltpu.VMEM((n_blk - 1, 8, width), f32),
            pltpu.VMEM((halves, width, HALF), bf16),
            pltpu.VMEM((n_dev - 1, CHUNK, HALF), bf16),
            pltpu.VMEM((CHUNK, HALF), f32),
            pltpu.VMEM((owners, CHUNK, HALF), f32),
            dma((4,)),
            dma((4,)),
            dma((n_slot,)),
            dma((halves,)),
            dma((halves,)),
            dma((halves,)),
            dma((halves,)),
            dma((halves, n_slot, n_rep)),
            dma((halves, n_slot, n_rep)),
            dma((halves, n_rep)),
            dma((halves, n_rep)),
            dma((halves, n_rep)),
            dma((halves, n_rep)),
            dma((halves, n_slot, n_rep)),
            dma((halves, n_slot * n_rep)),
            dma,
            dma,
            dma,
            dma,
            dma((n_blk,)),
            dma((owners,)),
        ],
        compiler_params=pltpu.CompilerParams(
            collective_id=0, has_side_effects=True, vmem_limit_bytes=56 * 2 ** 20
        ),
        name="graph_layer",
    )(inv, feats, weight, bias.reshape(1, width), grad_out, tile_values.reshape(n_slot * cells, tile, tile))
    out, gf, gw, gb = pl.pallas_call(
        deliver_kernel,
        out_shape=shapes,
        in_specs=[vmem] * 4,
        out_specs=(vmem,) * 4,
        name="deliver",
    )(*results)
    return (out, gf, gw, gb.reshape(width))


def solution(mesh):
    in_specs = (
        P(("blk", "rep"), None),
        P(),
        P(),
        P(("blk", "rep"), None),
        P("blk", "rep", None, None, None, None),
        P("blk", "rep", None, None),
        P("blk", "rep", None, None),
        P("blk", "rep", None),
    )
    out_specs = (P(("blk", "rep"), None), P(("blk", "rep"), None), P("rep", None), P())
    return jax.shard_map(body, mesh=mesh, in_specs=in_specs, out_specs=out_specs, check_vma=False)
```

```python
import functools

import jax
import jax.numpy as jnp
from jax import lax
from jax.experimental import pallas as pl
from jax.experimental.pallas import tpu as pltpu
from jax.sharding import PartitionSpec as P

MESH = pl.DeviceIdType.MESH
UNIT = 256
CHUNK = 16
HALF = 128


def remote(src, dst, send, recv, blk, rep):
    return pltpu.make_async_remote_copy(
        src_ref=src, dst_ref=dst, send_sem=send, recv_sem=recv, device_id=(blk, rep), device_id_type=MESH
    )


def layer_kernel(
    n_blk, n_rep, n_slot, tile, cells, tiles_side,
    count_ref, rows_hbm, cols_hbm, feats_hbm, weight_hbm, bias_hbm, gout_hbm, tiles_hbm,
    out_hbm, gf_hbm, gw_hbm, gb_hbm,
    rows_ref, cols_ref, inv_vec, inv_ref, feats_ref, weight_ref, bias_ref, gout_ref, out_ref, gf_ref, gw_ref, gb_ref,
    tiles, dense, dense_t, hw, hw_other, hwbuf, acc, part, aggbuf, gbuf, pbuf, ghbuf, feats_t,
    cross, bias_mine, bias_buf, terms, wbuf, wsum, fin,
    in_sem, index_sem, out_sem, tile_sem, swap_send, swap_recv, cross_send, cross_recv, hw_send, hw_recv,
    rs_send, rs_recv, ag_send, ag_recv, bw_send, bw_recv,
    bias_send, bias_recv, w_send, w_recv, fin_send, fin_recv,
):
    n_dev = n_blk * n_rep
    rows, width = feats_ref.shape
    units = rows * n_rep // UNIT
    per = UNIT // rows
    w_rows = width // n_rep
    halves = width // HALF
    groups = w_rows // CHUNK
    owners = groups * halves
    f32, bf16 = jnp.float32, jnp.bfloat16
    me_b = lax.axis_index("blk")
    me_r = lax.axis_index("rep")
    me = me_b * n_rep + me_r
    half = me_b // n_rep
    place = lax.rem(me_b, n_rep)
    partner = lax.rem(me_b + n_rep, n_blk)
    near_slot = jnp.where(place < me_r, 1, 0)

    def columns(c):
        return slice(c * HALF, (c + 1) * HALF)

    def unless(i, task):
        if i == 0:
            pl.when(me_r != 0)(task)
        else:
            task()

    index_in = [
        pltpu.make_async_copy(rows_hbm, rows_ref, index_sem.at[0]),
        pltpu.make_async_copy(cols_hbm, cols_ref, index_sem.at[1]),
    ]
    for copy in index_in:
        copy.start()
    small = []
    for i, (src, dst) in enumerate(
        ((feats_hbm, feats_ref), (weight_hbm, weight_ref), (bias_hbm, bias_ref), (gout_hbm, gout_ref))
    ):
        small.append(pltpu.make_async_copy(src, dst, in_sem.at[i]))
        small[-1].start()
    loads = []
    for k in range(n_slot):
        span = pl.ds(k * cells, cells)
        load = pltpu.make_async_copy(tiles_hbm.at[span], tiles.at[span], tile_sem.at[k])
        load.start()
        loads.append(load)
    barrier = pltpu.get_barrier_semaphore()

    def greet(d, carry):
        other = lax.rem(me + d, n_dev)
        pl.semaphore_signal(
            barrier, inc=1, device_id=(other // n_rep, lax.rem(other, n_rep)), device_id_type=MESH
        )
        return carry

    lax.fori_loop(1, n_dev, greet, 0)

    small[0].wait()
    small[1].wait()
    first = jnp.dot(feats_ref[...], weight_ref[...], preferred_element_type=f32).astype(bf16)
    for c in range(halves):
        hw[c] = first[:, columns(c)]

    for copy in index_in:
        copy.wait()
    for k in range(n_slot):
        named = rows_ref[k:k + 1] * tiles_side + cols_ref[k:k + 1]
        position = lax.broadcasted_iota(jnp.int32, (1, cells), 1)
        named = jnp.where(position < count_ref[k], named, -1)
        named = jnp.concatenate([named] * (HALF // cells), axis=1)
        by_entry = jnp.broadcast_to(named, (HALF, HALF)).T
        entry = lax.broadcasted_iota(jnp.int32, (HALF, HALF), 0)
        cell = lax.broadcasted_iota(jnp.int32, (HALF, HALF), 1)
        found = jnp.where(by_entry == cell, lax.rem(entry, cells) + k * cells, n_slot * cells)
        inv_vec[k:k + 1] = jnp.min(found, axis=0, keepdims=True)
    to_scalars = pltpu.make_async_copy(inv_vec, inv_ref, index_sem.at[2])
    to_scalars.start()
    pl.semaphore_wait(barrier, n_dev - 1)

    swaps = [
        remote(hw.at[c], hw_other.at[c], swap_send.at[c], swap_recv.at[c], partner, me_r) for c in range(halves)
    ]

    def hw_copy(c, h, r):
        to = half * n_rep + lax.rem(place + r, n_rep)
        src = hw if h == 0 else hw_other
        return remote(src.at[c], hwbuf.at[c, h, me_r], hw_send.at[c, h, r], hw_recv.at[c, h, me_r], to, r)

    def hw_share(c, h):
        for r in reversed(range(n_rep)):
            unless(r, lambda: hw_copy(c, h, r).start())

        @pl.when(me_r == 0)
        def _():
            hwbuf[c, h, 0] = hw[c] if h == 0 else hw_other[c]

    def fill(h):
        slot = jnp.where(near_slot == 1, 1 - h, h)

        def fill_rows(r, carry):
            at = pl.ds(pl.multiple_of(r * tile, tile), tile)
            for c in range(tiles_side):
                dense[h, at, c * tile:(c + 1) * tile] = tiles[inv_ref[slot, r * tiles_side + c]]
            return carry

        lax.fori_loop(0, tiles_side, fill_rows, 0)

    def fill_transposed(h):
        slot = jnp.where(near_slot == 1, 1 - h, h)

        def fill_rows(c, carry):
            at = pl.ds(pl.multiple_of(c * tile, tile), tile)
            for r in range(tiles_side):
                dense_t[h, at, r * tile:(r + 1) * tile] = tiles[inv_ref[slot, r * tiles_side + c]].T
            return carry

        lax.fori_loop(0, tiles_side, fill_rows, 0)

    for c in range(halves):
        swaps[c].start()
        if c == 0:
            hw_share(0, 0)
    tiles[n_slot * cells] = jnp.zeros((tile, tile), bf16)
    for load in loads:
        load.wait()
    to_scalars.wait()
    fill(0)
    swaps[0].wait_recv()
    hw_share(0, 1)
    for c in range(1, halves):
        hw_share(c, 0)
    fill(1)
    for c in range(1, halves):
        swaps[c].wait_recv()
        hw_share(c, 1)
    fill_transposed(1)

    def hw_wait(c, h, src):
        remote(
            hw.at[c], hwbuf.at[c, h, src], hw_send.at[c, h, src], hw_recv.at[c, h, src], me_b, me_r
        ).wait_recv()

    def rs_copy(c, j):
        return remote(part.at[c, j], aggbuf.at[c, me_r], rs_send.at[c, j], rs_recv.at[c, me_r], me_b, j)

    def forward(c):
        for h in range(2):
            for src in range(n_rep):
                unless(src, lambda: hw_wait(c, h, src))
            source = hwbuf[c, h].reshape(rows * n_rep, HALF)
            for j in range(units):
                at = slice(j * UNIT, (j + 1) * UNIT)
                got = jnp.dot(dense[h, at], source, preferred_element_type=f32)
                if h == 0:
                    acc[c, at] = got
                else:
                    got = got + acc[c, at]
                    acc[c, at] = got
                    part[c, j * per:(j + 1) * per] = got.astype(bf16).reshape(per, rows, HALF)
                    for i in range(j * per, (j + 1) * per):
                        pl.when(me_r != i)(lambda: rs_copy(c, i).start())

    def ag_copy(c, d):
        to = lax.rem(me_r + d, n_rep)
        return remote(
            gbuf.at[c, me_r], gbuf.at[c, me_r], ag_send.at[c, d], ag_recv.at[c, me_r], me_b, to
        )

    def activate(c):
        total = acc[c, pl.ds(pl.multiple_of(me_r * rows, rows), rows)]
        for d in range(1, n_rep):
            src = lax.rem(me_r + d, n_rep)
            remote(
                part.at[c, 0], aggbuf.at[c, src], rs_send.at[c, src], rs_recv.at[c, src], me_b, src
            ).wait_recv()
            total = total + aggbuf[c, src].astype(f32)
        pre = total + bias_ref[:, columns(c)]
        logistic = jax.nn.sigmoid(pre)
        cotangent = gout_ref[:, columns(c)].astype(f32)
        gbuf[c, me_r] = (cotangent * logistic * (1.0 + pre * (1.0 - logistic))).astype(bf16)
        for d in range(1, n_rep):
            ag_copy(c, d).start()
        out_ref[:, columns(c)] = (pre * logistic).astype(bf16)

    def bw_copy(c, h, j):
        to = half * n_rep + lax.rem(place - me_r + n_rep, n_rep)
        slot = h * n_rep + me_r
        return remote(pbuf.at[c, h, j], ghbuf.at[c, slot], bw_send.at[c, h, j], bw_recv.at[c, slot], to, j)

    def backward(c):
        for d in range(1, n_rep):
            src = lax.rem(me_r + d, n_rep)
            remote(
                gbuf.at[c, src], gbuf.at[c, src], ag_send.at[c, d], ag_recv.at[c, src], me_b, src
            ).wait_recv()
        grads = gbuf[c].reshape(rows * n_rep, HALF)
        for h in (1, 0):
            for u in range(units):
                term = jnp.dot(dense_t[h, u * UNIT:(u + 1) * UNIT], grads, preferred_element_type=f32)
                pbuf[c, h, u * per:(u + 1) * per] = term.astype(bf16).reshape(per, rows, HALF)
                for j in range(u * per, (u + 1) * per):
                    unless(j, lambda: bw_copy(c, h, j).start())
                    if j == 0:
                        @pl.when(me_r == 0)
                        def _():
                            ghbuf[c, h * n_rep] = pbuf[c, h, 0]
        bias_mine[:, columns(c)] = jnp.dot(
            jnp.ones((8, rows * n_rep), bf16), grads, preferred_element_type=f32
        )

    def arrived(c, slot):
        remote(
            pbuf.at[c, 0, 0], ghbuf.at[c, slot], bw_send.at[c, 0, 0], bw_recv.at[c, slot], me_b, me_r
        ).wait_recv()

    def summed(c, h):
        total = jnp.zeros((rows, HALF), f32)
        for r in range(n_rep):
            unless(r, lambda: arrived(c, h * n_rep + r))
            total = total + ghbuf[c, h * n_rep + r].astype(f32)
        return total

    overs = [
        remote(cross.at[c], ghbuf.at[c, 2 * n_rep], cross_send.at[c], cross_recv.at[c], partner, me_r)
        for c in range(halves)
    ]

    def send_over(c):
        cross[c] = summed(c, 1).astype(bf16)
        overs[c].start()

    def w_copy(c, g, r):
        to = (g * halves + c) * n_rep + r
        slot = lax.rem(me - to + n_dev, n_dev) - 1
        at = r * w_rows + g * CHUNK
        return remote(
            terms.at[c, at:at + CHUNK], wbuf.at[slot], w_send, w_recv, g * halves + c, r
        )

    def owned(c):
        total = summed(c, 0)
        overs[c].wait_recv()
        gh = (total + ghbuf[c, 2 * n_rep].astype(f32)).astype(bf16)
        terms[c] = jnp.dot(feats_t[...], gh, preferred_element_type=f32).astype(bf16)
        for g in range(groups):
            for r in range(n_rep):
                pl.when(me != (g * halves + c) * n_rep + r)(lambda: w_copy(c, g, r).start())
        return lax.dot_general(
            gh, weight_ref[:, columns(c)], (((1,), (1,)), ((), ())), preferred_element_type=f32
        )

    for c in range(halves):
        forward(c)
        if c == 0:
            fill_transposed(0)
            feats_t[...] = feats_ref[...].T
    small[2].wait()
    small[3].wait()
    for c in range(halves):
        activate(c)
    results = [
        pltpu.make_async_copy(src, dst, out_sem.at[i])
        for i, (src, dst) in enumerate(
            ((out_ref, out_hbm), (gf_ref, gf_hbm), (gw_ref, gw_hbm), (gb_ref, gb_hbm))
        )
    ]
    results[0].start()
    for c in range(halves):
        backward(c)

    def bias_send_one(d, carry):
        to = lax.rem(me_b + d, n_blk)
        remote(bias_mine, bias_buf.at[n_blk - 1 - d], bias_send, bias_recv, to, me_r).start()
        return carry

    lax.fori_loop(1, n_blk, bias_send_one, 0)

    for c in range(halves):
        send_over(c)
    feat_grad = owned(0)
    for c in range(1, halves):
        feat_grad = feat_grad + owned(c)
    gf_ref[...] = feat_grad.astype(bf16)
    results[1].start()
    remote(bias_buf, bias_buf, bias_send, bias_recv, me_b, me_r).wait_recv()
    gb_ref[...] = (bias_mine[...] + jnp.sum(bias_buf[...], axis=0))[0:1]
    results[3].start()

    def fin_copy(d):
        to = lax.rem(me_b + d, n_blk)
        return remote(wsum, fin.at[me_b], fin_send.at[d], fin_recv.at[me_b], to, me_r)

    def own_chunk():
        remote(wbuf, wbuf, w_send, w_recv, me_b, me_r).wait_recv()
        mine = terms[
            lax.rem(me_b, halves), pl.ds(pl.multiple_of(me_r * w_rows + me_b // halves * CHUNK, CHUNK), CHUNK)
        ]
        wsum[...] = mine.astype(f32) + jnp.sum(wbuf[...].astype(f32), axis=0)
        for d in range(1, n_blk):
            fin_copy(d).start()
        fin[me_b] = wsum[...]

    if owners == n_blk:
        own_chunk()
    else:
        pl.when(me_b < owners)(own_chunk)
    for o in range(owners):
        @pl.when(me_b != o)
        def _():
            remote(wsum, fin.at[o], fin_send.at[0], fin_recv.at[o], me_b, me_r).wait_recv()

        at = o // halves * CHUNK
        gw_ref[at:at + CHUNK, columns(o % halves)] = fin[o]
    results[2].start()

    for c in range(halves):
        swaps[c].wait_send()
        overs[c].wait_send()
        for h in range(2):
            for r in range(n_rep):
                unless(r, lambda: hw_copy(c, h, r).wait_send())
                unless(r, lambda: bw_copy(c, h, r).wait_send())
        for j in range(n_rep):
            pl.when(me_r != j)(lambda: rs_copy(c, j).wait_send())
        for d in range(1, n_rep):
            ag_copy(c, d).wait_send()
    remote(bias_buf, bias_buf, bias_send, bias_recv, me_b, me_r).wait_send()
    if owners == n_blk:
        remote(wbuf, wbuf, w_send, w_recv, me_b, me_r).wait_send()
    else:
        for c in range(halves):
            for g in range(groups):
                for r in range(n_rep):
                    pl.when(me != (g * halves + c) * n_rep + r)(lambda: w_copy(c, g, r).wait_send())

    def fin_left():
        for d in range(1, n_blk):
            fin_copy(d).wait_send()

    if owners == n_blk:
        fin_left()
    else:
        pl.when(me_b < owners)(fin_left)
    for result in results:
        result.wait()


def deliver_kernel(*refs):
    count = len(refs) // 2
    for src, dst in zip(refs[:count], refs[count:]):
        dst[...] = src[...]


def body(feats, weight, bias, grad_out, tile_values, tile_rows, tile_cols, tile_count):
    n_blk = lax.axis_size("blk")
    n_rep = lax.axis_size("rep")
    n_slot, cells, tile = tile_values.shape[2:5]
    rows, width = feats.shape
    n_dev = n_blk * n_rep
    part_rows = rows * n_rep
    side = part_rows // tile
    w_rows = width // n_rep
    owners = (w_rows // CHUNK) * (width // HALF)

    assert n_slot == 2 and n_blk == 2 * n_rep and HALF % cells == 0 and side * side <= HALF
    bf16, f32 = jnp.bfloat16, jnp.float32
    halves = width // HALF
    vmem = pl.BlockSpec(memory_space=pltpu.VMEM)
    anywhere = pl.BlockSpec(memory_space=pl.ANY)
    dma = pltpu.SemaphoreType.DMA
    shapes = (
        jax.ShapeDtypeStruct((rows, width), bf16),
        jax.ShapeDtypeStruct((rows, width), bf16),
        jax.ShapeDtypeStruct((w_rows, width), f32),
        jax.ShapeDtypeStruct((1, width), f32),
    )
    results = pl.pallas_call(
        functools.partial(layer_kernel, n_blk, n_rep, n_slot, tile, cells, side),
        out_shape=shapes,
        in_specs=[pl.BlockSpec(memory_space=pltpu.SMEM)] + [anywhere] * 7,
        out_specs=(anywhere,) * 4,
        scratch_shapes=[
            pltpu.VMEM((n_slot, cells), jnp.int32),
            pltpu.VMEM((n_slot, cells), jnp.int32),
            pltpu.VMEM((n_slot, HALF), jnp.int32),
            pltpu.SMEM((n_slot, HALF), jnp.int32),
            pltpu.VMEM((rows, width), bf16),
            pltpu.VMEM((width, width), bf16),
            pltpu.VMEM((1, width), f32),
            pltpu.VMEM((rows, width), bf16),
            pltpu.VMEM((rows, width), bf16),
            pltpu.VMEM((rows, width), bf16),
            pltpu.VMEM((w_rows, width), f32),
            pltpu.VMEM((1, width), f32),
            pltpu.VMEM((n_slot * cells + 1, tile, tile), bf16),
            pltpu.VMEM((n_slot, part_rows, part_rows), bf16),
            pltpu.VMEM((n_slot, part_rows, part_rows), bf16),
            pltpu.VMEM((halves, rows, HALF), bf16),
            pltpu.VMEM((halves, rows, HALF), bf16),
            pltpu.VMEM((halves, n_slot, n_rep, rows, HALF), bf16),
            pltpu.VMEM((halves, part_rows, HALF), f32),
            pltpu.VMEM((halves, n_rep, rows, HALF), bf16),
            pltpu.VMEM((halves, n_rep, rows, HALF), bf16),
            pltpu.VMEM((halves, n_rep, rows, HALF), bf16),
            pltpu.VMEM((halves, n_slot, n_rep, rows, HALF), bf16),
            pltpu.VMEM((halves, n_slot * n_rep + 1, rows, HALF), bf16),
            pltpu.VMEM((width, rows), bf16),
            pltpu.VMEM((halves, rows, HALF), bf16),
            pltpu.VMEM((8, width), f32),
            pltpu.VMEM((n_blk - 1, 8, width), f32),
            pltpu.VMEM((halves, width, HALF), bf16),
            pltpu.VMEM((n_dev - 1, CHUNK, HALF), bf16),
            pltpu.VMEM((CHUNK, HALF), f32),
            pltpu.VMEM((owners, CHUNK, HALF), f32),
            dma((4,)),
            dma((3,)),
            dma((4,)),
            dma((n_slot,)),
            dma((halves,)),
            dma((halves,)),
            dma((halves,)),
            dma((halves,)),
            dma((halves, n_slot, n_rep)),
            dma((halves, n_slot, n_rep)),
            dma((halves, n_rep)),
            dma((halves, n_rep)),
            dma((halves, n_rep)),
            dma((halves, n_rep)),
            dma((halves, n_slot, n_rep)),
            dma((halves, n_slot * n_rep)),
            dma,
            dma,
            dma,
            dma,
            dma((n_blk,)),
            dma((owners,)),
        ],
        compiler_params=pltpu.CompilerParams(
            collective_id=0, has_side_effects=True, vmem_limit_bytes=56 * 2 ** 20
        ),
        name="graph_layer",
    )(
        tile_count[0, 0], tile_rows[0, 0], tile_cols[0, 0], feats, weight, bias.reshape(1, width), grad_out,
        tile_values.reshape(n_slot * cells, tile, tile),
    )
    out, gf, gw, gb = pl.pallas_call(
        deliver_kernel,
        out_shape=shapes,
        in_specs=[vmem] * 4,
        out_specs=(vmem,) * 4,
        name="deliver",
    )(*results)
    return (out, gf, gw, gb.reshape(width))


def solution(mesh):
    in_specs = (
        P(("blk", "rep"), None),
        P(),
        P(),
        P(("blk", "rep"), None),
        P("blk", "rep", None, None, None, None),
        P("blk", "rep", None, None),
        P("blk", "rep", None, None),
        P("blk", "rep", None),
    )
    out_specs = (P(("blk", "rep"), None), P(("blk", "rep"), None), P("rep", None), P())
    return jax.shard_map(body, mesh=mesh, in_specs=in_specs, out_specs=out_specs, check_vma=False)
```
